256 devices in a mesh: ex: 32 (over y, z), tp: 8 (over x, core).
Axes of the slice: x: 4, y: 4, z: 8, core: 2. Of those that a mesh axis runs over, the one named last changes fastest.
Arguments:
- down_matrix_feeds: bfloat16 [32768, 28672], P('ex', 'tp'), may hold values from -6 to 6
- result_slope_matrix: bfloat16 [32768, 8192], P('ex', 'tp'), may hold values from -6 to 6
- feed_sketch_factor: bfloat16 [28672, 64], P('tp'), may hold values from -0.03125 to 0.03125
- result_slope_factor: bfloat16 [8192, 64], P('tp'), may hold values from -0.0625 to 0.0625
- heldout_slope_entries: bfloat16 [2048, 4096], P('ex', 'tp'), may hold values from -0.01171875 to 0.01171875
- objective_of_sample: int32 [512], P('ex'), may hold values from 0 to 2047
- kept_choice_flags: int32 [2048], replicated, may hold values 0 or 1
- token_sample_position: int32 [32, 1024], P('ex'), may hold values from 0 to 15, never falling along the last dimension, each value on 1 to 128 neighbouring positions
Outputs:
- sample_affinity: float32 [512, 2048], P('ex')
- totals: float32 [2048], P('ex')
The draws below stay inside these ranges and needn't reach their ends.
Inputs may be any that keep to these rules, and one draw needn't show every extreme that they name: `token_sample_position`: each row runs from 0 to 15 without falling; each example has 1 to 128 tokens, and one of each row has exactly 128.
All inputs are finite; a program needn't handle non-finite values.
Results may differ from the reference program's by a relative error of at most 0.0031.
Values may be sent and summed in bfloat16 or wider, within the bound.
No kernel may reach another device: no remote copies, remote signals or barrier semaphores. Data moves between devices by JAX's collectives and lax.ppermute only.
A program may use at most 128 MiB of HBM per device.

```python
import math
import jax
import jax.numpy as jnp
import numpy as np
from jax import lax

D = 8192
FF = 28672
RANK = 64
TOK_DEV = 1024
E_DEV = 16
MOST = 128
OBJECTIVE_CHOICE = 2048
TOKENS = 32768
EXAMPLES = 512
N_EX = 32


def set_ends(values, key, low, largest):
    dims = values.shape
    index_at = [jax.random.randint(jax.random.fold_in(key, axis), (), 0, dims[axis]) for axis in range(len(dims))]
    values = values.at[tuple(index_at)].set(low)
    longest = dims.index(max(dims))
    index_at[longest] = (index_at[longest] + 1) % dims[longest]
    return values.at[tuple(index_at)].set(largest)


def steps_of(own_key, dims, cuts, low, high):
    level, own = 1.0, jax.random.fold_in(own_key, 6)
    for position, parts in cuts:
        heights = jnp.exp(jax.random.uniform(jax.random.fold_in(own, position), (parts,), jnp.float32, low / len(cuts), high / len(cuts)))
        level = level * jnp.repeat(heights, dims[position] // parts).reshape([-1 if axis == position else 1 for axis in range(len(dims))])
    return level


def split_up(amount, total, bound, lean):
    loads = [(1 << 20) // math.isqrt(standing ** lean) + 1 for standing in range(2, amount + 1)]
    surplus, given = total - bound - (amount - 1), [1] * (amount - 1)
    while surplus > 0:
        free = [i for i in range(amount - 1) if given[i] < bound]
        mass, left = sum([loads[i] for i in free]), surplus
        for i in free:
            more = min(bound - given[i], max(1, left * loads[i] // mass), surplus)
            given[i] = given[i] + more
            surplus = surplus - more
    return np.array([bound] + given)


def ragged_sizes(own_key, number_of, total, limit, slope):
    if number_of == 2:
        one = jax.random.randint(own_key, (), max(1, total - limit), min(limit, total - 1) + 1)
        return jnp.stack([one, total - one])
    lengths = jnp.asarray(split_up(number_of, total, limit, slope), jnp.int32)
    couples = (number_of - 1) // 2
    source_of, receiver = lengths[1:1 + 2 * couples:2], lengths[2:2 + 2 * couples:2]
    margin = jnp.minimum(source_of - 1, limit - receiver)
    passed = jax.random.randint(jax.random.fold_in(own_key, 1), (couples,), 0, 1 << 20) % (margin + 1)
    lengths = lengths.at[1:1 + 2 * couples:2].set(source_of - passed).at[2:2 + 2 * couples:2].set(receiver + passed)
    return lengths[jax.random.permutation(jax.random.fold_in(own_key, 2), number_of)]


def normal_values(stream_key, dims, spread, most, cuts=(), kind=jnp.bfloat16):
    result = jax.random.normal(stream_key, dims, jnp.float32) * spread
    if len(cuts) > 0:
        result = steps_of(stream_key, dims, cuts, -0.22, 0.18) * result
    return jnp.clip(result, min=-most, max=most).astype(kind)


def setup_inputs(seed: int = 0) -> dict:
    key_list = jax.random.split(jax.random.key(seed), 9)
    down_matrix_feeds = normal_values(key_list[0], (TOKENS, FF), 1.0, 6.0, ((0, 32), (1, 8)))
    result_slope_matrix = normal_values(key_list[1], (TOKENS, D), 1.0, 6.0, ((0, 32), (1, 8)))
    feed_sketch_factor = normal_values(key_list[2], (FF, RANK), FF ** -0.5, 0.03125, ((0, 8),))
    result_slope_factor = normal_values(key_list[3], (D, RANK), D ** -0.5, 0.0625, ((0, 8),))
    heldout_slope_entries = normal_values(key_list[4], (OBJECTIVE_CHOICE, RANK * RANK), (RANK * RANK * TOK_DEV // E_DEV) ** -0.5, 0.01171875, ((0, 32), (1, 8)))
    objective_of_sample = set_ends(jax.random.randint(key_list[5], (EXAMPLES,), 0, OBJECTIVE_CHOICE), jax.random.fold_in(key_list[5], 1), 0, OBJECTIVE_CHOICE - 1).astype(jnp.int32)
    kept_choice_flags = set_ends((jax.random.randint(key_list[6], (OBJECTIVE_CHOICE,), 0, 4) < 3).astype(jnp.int32), jax.random.fold_in(key_list[6], 1), 0, 1)
    token_sample_position = jax.vmap(lambda own: jnp.searchsorted(jnp.cumsum(ragged_sizes(own, E_DEV, TOK_DEV, MOST, 0)), jnp.arange(TOK_DEV), side="right"))(jax.random.split(key_list[7], N_EX)).reshape((N_EX, TOK_DEV)).astype(jnp.int32)
    return dict(down_matrix_feeds=down_matrix_feeds, result_slope_matrix=result_slope_matrix, feed_sketch_factor=feed_sketch_factor, result_slope_factor=result_slope_factor, heldout_slope_entries=heldout_slope_entries, objective_of_sample=objective_of_sample, kept_choice_flags=kept_choice_flags, token_sample_position=token_sample_position)


def reference(down_matrix_feeds, result_slope_matrix, feed_sketch_factor, result_slope_factor, heldout_slope_entries, objective_of_sample, kept_choice_flags, token_sample_position):
    in_low = jnp.dot(down_matrix_feeds, feed_sketch_factor, preferred_element_type=jnp.float32)
    out_low = jnp.dot(result_slope_matrix, result_slope_factor, preferred_element_type=jnp.float32)
    in_shards = in_low.reshape(N_EX, TOK_DEV, RANK)
    out_shards = out_low.reshape(N_EX, TOK_DEV, RANK)

    def one_shard(items):
        in_rows, out_rows, seg_row = items
        labels = lax.broadcasted_iota(jnp.int32, (E_DEV, TOK_DEV), 0)
        onehot = (seg_row[None, :] == labels).astype(jnp.float32)
        weighted = onehot[:, None, :] * in_rows.T[None, :, :]
        grads = jnp.einsum("eit,tj->eij", weighted, out_rows, precision=lax.Precision.HIGHEST)
        return grads.reshape(E_DEV, RANK * RANK)

    per_example = lax.map(one_shard, (in_shards, out_shards, token_sample_position))
    per_example = per_example.reshape(EXAMPLES, RANK * RANK).astype(jnp.bfloat16)
    raw_affinity = lax.dot_general(per_example, heldout_slope_entries, (((1,), (1,)), ((), ())), preferred_element_type=jnp.float32)
    sample_affinity = raw_affinity * kept_choice_flags.astype(jnp.float32)[None, :]
    columns = lax.broadcasted_iota(jnp.int32, (EXAMPLES, OBJECTIVE_CHOICE), 1)
    chosen = (objective_of_sample[:, None] == columns).astype(jnp.float32)
    totals = jnp.sum(chosen * sample_affinity, axis=0)
    return sample_affinity, totals
```

```python
import jax
import jax.numpy as jnp
from jax import lax
from jax.sharding import PartitionSpec as P

NY, NZ, NX = 4, 8, 4
F32, BF16 = jnp.float32, jnp.bfloat16


def tp_swap(value, bits):
    return lax.ppermute(value, "tp", [(i, i ^ bits) for i in range(2 * NX)])


def y_swap(value, bits):
    return lax.ppermute(value, "ex", [(i, i ^ (bits * NZ)) for i in range(NY * NZ)])


def z_shift(value, step):
    return lax.ppermute(
        value, "ex", [(y * NZ + z, y * NZ + (z + step) % NZ) for y in range(NY) for z in range(NZ)]
    )


def split_two(value):
    high = lax.reduce_precision(value, 8, 7)
    return high.astype(BF16), (value - high).astype(BF16)


def pick(pair, index):
    return jnp.where(index == 0, pair[0], pair[1])


def per_device(
    down_matrix_feeds,
    result_slope_matrix,
    feed_sketch_factor,
    result_slope_factor,
    heldout_slope_entries,
    objective_of_sample,
    kept_choice_flags,
    token_sample_position,
):
    tokens = down_matrix_feeds.shape[0]
    rank = feed_sketch_factor.shape[1]
    examples = objective_of_sample.shape[0]
    choices = kept_choice_flags.shape[0]
    own_choices = heldout_slope_entries.shape[0]
    tp, ex = lax.axis_index("tp"), lax.axis_index("ex")
    x, core, y, z = tp // 2, tp % 2, ex // NZ, ex % NZ

    held = jnp.stack([heldout_slope_entries] + [y_swap(heldout_slope_entries, d) for d in (1, 2, 3)])
    up = down = held
    blocks = {0: held}
    for step in range(1, NZ // 2 + 1):
        up = z_shift(up, 1)
        blocks[step] = up
        if step < NZ // 2:
            down = z_shift(down, -1)
            blocks[NZ - step] = down

    nt = (((0,), (1,)), ((), ()))
    in_part = lax.dot_general(feed_sketch_factor, down_matrix_feeds, nt, preferred_element_type=F32)
    out_part = lax.dot_general(result_slope_factor, result_slope_matrix, nt, preferred_element_type=F32)

    rows = rank // (2 * NX)
    in_cores = in_part.reshape(NX, 2, rows, tokens)
    in_cores = (in_cores[:, 0].reshape(NX * rows, tokens), in_cores[:, 1].reshape(NX * rows, tokens))
    out_cores = (out_part[: rank // 2], out_part[rank // 2 :])
    both = [jnp.concatenate([i, o], 0) for i, o in zip(in_cores, out_cores)]
    mine = pick(both, core) + tp_swap(pick(both, 1 - core), 1)
    in_chip, out_chip = mine[: NX * rows].reshape(NX, rows, tokens), mine[NX * rows :]
    out_sent = out_chip.astype(BF16)
    in_own = lax.dynamic_index_in_dim(in_chip, x, 0, False)
    got = []
    for d in (1, 2, 3):
        part = lax.dynamic_index_in_dim(in_chip, x ^ d, 0, False)
        got.append(tp_swap(jnp.concatenate([*split_two(part), out_sent], 0), 2 * d).astype(F32))
    in_sum = in_own + sum(g[:rows] + g[rows : 2 * rows] for g in got)
    out_half = out_chip + sum(g[2 * rows :] for g in got)
    out_other = tp_swap(out_half, 1)
    out_sum = jnp.where(core == 0, jnp.concatenate([out_half, out_other], 0), jnp.concatenate([out_other, out_half], 0))

    labels = lax.broadcasted_iota(jnp.int32, (examples, tokens), 0)
    onehot = (token_sample_position[0][None, :] == labels).astype(F32)
    weighted = (onehot[:, None, :] * in_sum[None, :, :]).reshape(examples * rows, tokens)
    grads = lax.dot_general(
        weighted, out_sum, (((1,), (1,)), ((), ())), precision=lax.Precision.HIGHEST, preferred_element_type=F32
    )
    per_example = jnp.concatenate(split_two(grads.reshape(examples, rows * rank)), 0)

    scores = []
    for k in range(NZ):
        block = blocks[k].reshape(NY * own_choices, -1)
        s = lax.dot_general(per_example, block, (((1,), (1,)), ((), ())), preferred_element_type=F32)
        scores.append((s[:examples] + s[examples:]).reshape(examples, NY, 1, own_choices))
    scores = scores[::-1]
    shift = z + 1
    for bit in (1, 2, 4):
        turned = [scores[(m - bit) % NZ] for m in range(NZ)]
        scores = [jnp.where((shift & bit) != 0, t, s) for t, s in zip(turned, scores)]
    scores = jnp.concatenate(scores, 2)
    for bit in (1, 2):
        turned = jnp.concatenate([scores[:, m ^ bit : (m ^ bit) + 1] for m in range(NY)], 1)
        scores = jnp.where((y & bit) != 0, turned, scores)
    scores = scores.reshape(examples, choices)

    halves = (scores[:, : choices // 2], scores[:, choices // 2 :])
    mine = pick(halves, core) + tp_swap(pick(halves, 1 - core), 1)
    mine = (mine + tp_swap(mine, 2)) + (tp_swap(mine, 4) + tp_swap(mine, 6))
    other = tp_swap(mine, 1)
    flags = kept_choice_flags.astype(F32)[None, :]
    sample_affinity = flags * jnp.where(
        core == 0, jnp.concatenate([mine, other], 1), jnp.concatenate([other, mine], 1)
    )

    columns = lax.broadcasted_iota(jnp.int32, (examples, choices), 1)
    chosen = (objective_of_sample[:, None] == columns).astype(F32)
    partial_totals = jnp.sum(chosen * sample_affinity, axis=0).reshape(NY * NZ, own_choices)
    totals = jnp.sum(lax.all_to_all(partial_totals, "ex", 0, 0, tiled=True), axis=0)
    return (sample_affinity, totals)


def solution(mesh):
    placed = (
        P("ex", "tp"),
        P("ex", "tp"),
        P("tp", None),
        P("tp", None),
        P("ex", "tp"),
        P("ex"),
        P(),
        P("ex", None),
    )
    return jax.shard_map(
        per_device, mesh=mesh, in_specs=placed, out_specs=(P("ex", None), P("ex")), check_vma=False
    )
```

```python
import jax
import jax.numpy as jnp
from jax import lax
from jax.experimental import pallas as pl
from jax.experimental.pallas import tpu as pltpu
from jax.sharding import Mesh
from jax.sharding import PartitionSpec as P

NY, NZ, NX, NC = 4, 8, 4, 2
SIZES = dict(y=NY, z=NZ, x=NX, core=NC)
RANK, TOK, E_DEV, C_DEV, K_DEV, CHOICES = 64, 1024, 16, 64, 512, 2048
ROWS = RANK // (NX * NC)
HALF = RANK // 2
E_ALL, C_ALL = NY * E_DEV, NZ * C_DEV
C_HALF = C_ALL // 2
F32, BF16, I32 = jnp.float32, jnp.bfloat16, jnp.int32
NT = (((1,), (1,)), ((), ()))
VMEM_LIMIT = 48 * 1024 * 1024


def swap(value, axis, bits):
    return lax.ppermute(value, axis, [(i, i ^ bits) for i in range(SIZES[axis])])


def shaped(*dims, dtype=F32):
    return jax.ShapeDtypeStruct(dims, dtype)


def call(body, outs, *args, scratch=()):
    return pl.pallas_call(
        body,
        out_shape=outs,
        scratch_shapes=scratch,
        compiler_params=pltpu.CompilerParams(vmem_limit_bytes=VMEM_LIMIT),
    )(*args)


def project_body(x_ref, y_ref, w_in_ref, w_out_ref, keep_ref, send_ref):
    core = lax.axis_index("core")
    low = lax.dot_general(w_in_ref[...], x_ref[...], NT, preferred_element_type=F32)
    out = lax.dot_general(w_out_ref[...], y_ref[...], NT, preferred_element_type=F32)
    for c in range(NC):
        part = [low[(NC * j + c) * ROWS : (NC * j + c + 1) * ROWS] for j in range(NX)]
        part = jnp.concatenate(part + [out[c * HALF : (c + 1) * HALF]], 0)

        @pl.when(core == c)
        def _():
            keep_ref[...] = part

        @pl.when(core != c)
        def _():
            send_ref[...] = part


def project(x, y, w_in, w_out):
    block = 256
    whole = lambda a: pl.BlockSpec(a.shape, lambda i: (0, 0))
    out = pl.BlockSpec((RANK, block), lambda i: (0, i))
    return pl.pallas_call(
        project_body,
        grid=(TOK // block,),
        in_specs=[
            pl.BlockSpec((block, x.shape[1]), lambda i: (i, 0)),
            pl.BlockSpec((block, y.shape[1]), lambda i: (i, 0)),
            whole(w_in),
            whole(w_out),
        ],
        out_specs=[out, out],
        out_shape=[shaped(RANK, TOK), shaped(RANK, TOK)],
        compiler_params=pltpu.CompilerParams(vmem_limit_bytes=VMEM_LIMIT),
    )(x, y, w_in, w_out)


def halves_of(value):
    high = value.astype(BF16)
    return high, (value - high.astype(F32)).astype(BF16)


def spread_body(keep_ref, got_ref, s1_ref, s2_ref, s3_ref, in_ref, out_ref):
    x = lax.axis_index("x")
    for d, ref in ((1, s1_ref), (2, s2_ref), (3, s3_ref), (0, None)):
        at = pl.ds(pl.multiple_of((x ^ d) * ROWS, ROWS), ROWS)
        part = keep_ref[at, :] + got_ref[at, :]
        if ref is None:
            in_ref[...] = part
        else:
            ref[: 2 * ROWS] = jnp.concatenate(halves_of(part), 0)
    out = keep_ref[NX * ROWS :] + got_ref[NX * ROWS :]
    out_ref[...] = out
    for ref in (s1_ref, s2_ref, s3_ref):
        ref[2 * ROWS :] = out.astype(BF16)


def outer_body(in_ref, g1_ref, g2_ref, g3_ref, mine_ref, other_ref, where_ref, goal_ref, p_ref):
    core = lax.axis_index("core")
    low = in_ref[...]
    for ref in (g1_ref, g2_ref, g3_ref):
        g = ref[: 2 * ROWS].astype(F32)
        low = low + (g[:ROWS] + g[ROWS:])
    mine, other = mine_ref[...], other_ref[...]
    out = jnp.concatenate([jnp.where(core == 0, mine, other), jnp.where(core == 0, other, mine)], 0)
    onehot = lax.broadcasted_iota(I32, (E_DEV, TOK), 0) == where_ref[...]
    weighted = jnp.concatenate([jnp.where(onehot, low[i : i + 1], 0.0) for i in range(ROWS)], 0)
    grads = lax.dot_general(weighted, out, NT, precision=lax.Precision.HIGHEST, preferred_element_type=F32)
    flat = jnp.concatenate([grads[i * E_DEV : (i + 1) * E_DEV] for i in range(ROWS)], 1)
    high, low = halves_of(flat)
    goal = jnp.broadcast_to(goal_ref[...], (E_DEV, 128))
    p_ref[:E_DEV, :K_DEV] = high
    p_ref[E_DEV:, :K_DEV] = low
    p_ref[:E_DEV, K_DEV:] = (goal >> 4).astype(F32).astype(BF16)
    p_ref[E_DEV:, K_DEV:] = (goal & 15).astype(F32).astype(BF16)


def score_body(p0, p1, p2, p3, h_ref, keep_ref, send_ref, goal_ref, held):
    core, z = lax.axis_index("core"), lax.axis_index("z")
    for m, bits in enumerate((0, 4, 2, 6, 1, 5, 3, 7)):
        held[pl.ds(pl.multiple_of((z ^ bits) * C_DEV, C_DEV), C_DEV), :] = h_ref[m]
    ps = [p[...] for p in (p0, p1, p2, p3)]
    left = jnp.concatenate([p[:E_DEV, :K_DEV] for p in ps] + [p[E_DEV:, :K_DEV] for p in ps], 0)
    score = lax.dot_general(left, held[...], NT, preferred_element_type=F32)
    score = score[:E_ALL] + score[E_ALL:]
    first, second = score[:, :C_HALF], score[:, C_HALF:]
    keep_ref[...] = jnp.where(core == 0, first, second)
    send_ref[...] = jnp.where(core == 0, second, first)
    goal = [p[:E_DEV, K_DEV:].astype(F32) * 16.0 + p[E_DEV:, K_DEV:].astype(F32) for p in ps]
    goal_ref[...] = jnp.concatenate(goal, 0)


def total_body(a0, a1, a2, a3, goal_ref, flag_ref, s0, s1, s2, s3, slots_ref):
    core, y = lax.axis_index("core"), lax.axis_index("y")
    score = (a0[...] + a1[...]) + (a2[...] + a3[...])
    score = score * flag_ref[pl.ds(y * NC + core, 1), :]
    for d, ref in enumerate((s0, s1, s2, s3)):
        ref[...] = score[d * E_DEV : (d + 1) * E_DEV]
    first = ((y * NC + core) * C_HALF).astype(F32)
    goal = goal_ref[...] - first
    lane = lax.broadcasted_iota(I32, (E_ALL, 128), 1).astype(F32)
    sums = [
        jnp.sum(jnp.where(goal == lane + 128.0 * j, score[:, 128 * j : 128 * (j + 1)], 0.0), 0, keepdims=True)
        for j in range(C_HALF // 128)
    ]
    slots_ref[...] = jnp.zeros_like(slots_ref)
    for j in range(C_HALF // C_DEV):
        piece = sums[j // 2][:, (j % 2) * C_DEV : (j % 2 + 1) * C_DEV]
        for c in range(NC):
            slots_ref[pl.ds((core * (NZ // NC) + j) * NC + c, 1), 0, :] = piece


def lay_body(mine_ref, other_ref, out_ref):
    core, y = lax.axis_index("core"), lax.axis_index("y")
    for d in range(NY):
        for part, ref in ((core, mine_ref), (1 - core, other_ref)):
            at = pl.multiple_of((y ^ d) * C_ALL + part * C_HALF, C_HALF)
            out_ref[:, pl.ds(at, C_HALF)] = ref[d * E_DEV : (d + 1) * E_DEV, :]


def per_device(
    down_matrix_feeds,
    result_slope_matrix,
    feed_sketch_factor,
    result_slope_factor,
    heldout_slope_entries,
    objective_of_sample,
    kept_choice_flags,
    token_sample_position,
):
    held = heldout_slope_entries[None]
    for bits in (4, 2, 1):
        held = jnp.concatenate([held, swap(held, "z", bits)], 0)

    keep, send = project(
        down_matrix_feeds, result_slope_matrix, feed_sketch_factor.T, result_slope_factor.T
    )
    sent = shaped(6 * ROWS, TOK, dtype=BF16)
    s1, s2, s3, in_own, out_chip = call(
        spread_body,
        [sent, sent, sent, shaped(ROWS, TOK), shaped(HALF, TOK)],
        keep,
        swap(send, "core", 1),
    )
    got = [swap(s, "x", d) for d, s in ((1, s1), (2, s2), (3, s3))]
    out_half = out_chip + sum(g[2 * ROWS :].astype(F32) for g in got)
    packed = call(
        outer_body,
        shaped(2 * E_DEV, K_DEV + 128, dtype=BF16),
        in_own,
        *got,
        out_half,
        swap(out_half, "core", 1),
        token_sample_position,
        objective_of_sample[:, None],
    )
    packs = [packed] + [swap(packed, "y", d) for d in (1, 2, 3)]

    half = shaped(E_ALL, C_HALF)
    keep, send, goal = call(
        score_body,
        [half, half, shaped(E_ALL, 128)],
        *packs,
        held,
        scratch=[pltpu.VMEM((C_ALL, K_DEV), BF16)],
    )
    mine = keep + swap(send, "core", 1)
    flags = kept_choice_flags.astype(F32).reshape(NY * NC, C_HALF)
    piece = shaped(E_DEV, C_HALF)
    *pieces, slots = call(
        total_body,
        [piece] * NY + [shaped(NZ * NC, 1, C_DEV)],
        mine,
        *[swap(mine, "x", d) for d in (1, 2, 3)],
        goal,
        flags,
    )
    mine = jnp.concatenate([pieces[0]] + [swap(pieces[d], "y", d) for d in (1, 2, 3)], 0)
    totals = jnp.sum(lax.all_to_all(slots, ("z", "core"), 0, 0, tiled=True), axis=(0, 1))
    sample_affinity = call(lay_body, shaped(E_DEV, CHOICES), mine, swap(mine, "core", 1))
    return (sample_affinity, totals)


def solution(mesh):
    ex, tp = ("y", "z"), ("x", "core")
    chips = Mesh(mesh.devices.reshape(NY, NZ, NX, NC), ("y", "z", "x", "core"))
    placed = (
        P(ex, tp),
        P(ex, tp),
        P(tp, None),
        P(tp, None),
        P(ex, tp),
        P(ex),
        P(),
        P(ex, None),
    )
    return jax.shard_map(
        per_device, mesh=chips, in_specs=placed, out_specs=(P(ex, None), P(ex)), check_vma=False
    )
```

```python
import jax
import jax.numpy as jnp
from jax import lax
from jax.experimental import pallas as pl
from jax.experimental.pallas import tpu as pltpu
from jax.sharding import Mesh
from jax.sharding import PartitionSpec as P

NY, NZ, NX, NC = 4, 8, 4, 2
SIZES = dict(y=NY, z=NZ, x=NX, core=NC)
RANK, TOK, E_DEV, C_DEV, K_DEV, CHOICES = 64, 1024, 16, 64, 512, 2048
ROWS = RANK // (NX * NC)
HALF = RANK // 2
E_ALL, C_ALL = NY * E_DEV, NZ * C_DEV
C_HALF = C_ALL // 2
F32, BF16, I32, I16 = jnp.float32, jnp.bfloat16, jnp.int32, jnp.int16
NT = (((1,), (1,)), ((), ()))
CHUNK = 512
VMEM_LIMIT = 48 * 1024 * 1024


def swap(value, axis, bits):
    return lax.ppermute(value, axis, [(i, i ^ bits) for i in range(SIZES[axis])])


def shaped(*dims, dtype=F32):
    return jax.ShapeDtypeStruct(dims, dtype)


def call(body, outs, *args, scratch=()):
    return pl.pallas_call(
        body,
        out_shape=outs,
        scratch_shapes=scratch,
        compiler_params=pltpu.CompilerParams(vmem_limit_bytes=VMEM_LIMIT),
    )(*args)


def project_body(x_hbm, y_hbm, w_in_hbm, w_out_hbm, keep_ref, send_ref, parts, w_in, w_out, low, out, sems):
    core = lax.axis_index("core")
    steps = [(y_hbm, w_out, out, k) for k in range(y_hbm.shape[1] // CHUNK)]
    steps += [(x_hbm, w_in, low, k) for k in range(x_hbm.shape[1] // CHUNK)]
    copies = [
        pltpu.make_async_copy(src.at[:, pl.ds(k * CHUNK, CHUNK)], parts.at[n], sems.at[n])
        for n, (src, _, _, k) in enumerate(steps)
    ]
    copy_out = pltpu.make_async_copy(w_out_hbm, w_out, sems.at[len(steps)])
    copy_in = pltpu.make_async_copy(w_in_hbm, w_in, sems.at[len(steps) + 1])
    copy_out.start()
    copies[0].start()
    copy_in.start()
    for copy in copies[1:]:
        copy.start()
    copy_out.wait()
    for n, (src, weights, total, k) in enumerate(steps):
        copies[n].wait()
        if src is x_hbm and k == 0:
            copy_in.wait()
        part = lax.dot_general(
            weights[:, k * CHUNK : (k + 1) * CHUNK], parts[n], NT, preferred_element_type=F32
        )
        if k == 0:
            total[...] = part
        else:
            total[...] += part
    for c in range(NC):
        part = [low[(NC * j + c) * ROWS : (NC * j + c + 1) * ROWS] for j in range(NX)]
        part = jnp.concatenate(part + [out[c * HALF : (c + 1) * HALF]], 0)

        @pl.when(core == c)
        def _():
            keep_ref[...] = part

        @pl.when(core != c)
        def _():
            send_ref[...] = part


def project(x, y, w_in, w_out):
    steps = (x.shape[1] + y.shape[1]) // CHUNK
    args = [pltpu.with_memory_space_constraint(a, pltpu.HBM) for a in (x, y, w_in, w_out)]
    return pl.pallas_call(
        project_body,
        in_specs=[pl.BlockSpec(memory_space=pltpu.HBM)] * 4,
        out_shape=[shaped(RANK, TOK), shaped(RANK, TOK)],
        scratch_shapes=[
            pltpu.VMEM((steps, TOK, CHUNK), BF16),
            pltpu.VMEM(w_in.shape, BF16),
            pltpu.VMEM(w_out.shape, BF16),
            pltpu.VMEM((RANK, TOK), F32),
            pltpu.VMEM((RANK, TOK), F32),
            pltpu.SemaphoreType.DMA((steps + 2,)),
        ],
        compiler_params=pltpu.CompilerParams(vmem_limit_bytes=VMEM_LIMIT),
    )(*args)


def coded(value):
    top = jnp.maximum(jnp.max(jnp.abs(value), 0, keepdims=True), 1e-30)
    power = jnp.clip(jnp.floor(jnp.log2(top)) - 13.0, -100.0, 100.0)
    return jnp.round(value / jnp.exp2(power)), power


def spread_body(keep_ref, got_ref, s1_ref, s2_ref, s3_ref, in_ref, out_ref):
    x = lax.axis_index("x")
    out = keep_ref[NX * ROWS :] + got_ref[NX * ROWS :]
    out_ref[...] = out
    out_code, out_power = coded(out)
    line = lax.broadcasted_iota(I32, (ROWS, TOK), 0)
    for d, ref in ((1, s1_ref), (2, s2_ref), (3, s3_ref), (0, None)):
        at = pl.ds(pl.multiple_of((x ^ d) * ROWS, ROWS), ROWS)
        part = keep_ref[at, :] + got_ref[at, :]
        if ref is None:
            in_ref[...] = part
        else:
            code, power = coded(part)
            powers = jnp.where(line == 0, power, out_power)
            ref[...] = jnp.concatenate([code, out_code, powers], 0).astype(I32).astype(I16)


def add_body(in_ref, out_ref, g1_ref, g2_ref, g3_ref, low_ref, half_ref):
    low, half = in_ref[...], out_ref[...]
    for ref in (g1_ref, g2_ref, g3_ref):
        got = ref[...].astype(I32).astype(F32)
        powers = jnp.exp2(got[ROWS + HALF :])
        low = low + got[:ROWS] * powers[:1]
        half = half + got[ROWS : ROWS + HALF] * powers[1:2]
    low_ref[...] = low
    half_ref[...] = half


def outer_body(in_ref, mine_ref, other_ref, where_ref, goal_ref, p_ref):
    core = lax.axis_index("core")
    low, mine, other = in_ref[...], mine_ref[...], other_ref[...]
    out = jnp.concatenate([jnp.where(core == 0, mine, other), jnp.where(core == 0, other, mine)], 0)
    onehot = lax.broadcasted_iota(I32, (E_DEV, TOK), 0) == where_ref[...]
    weighted = jnp.concatenate([jnp.where(onehot, low[i : i + 1], 0.0) for i in range(ROWS)], 0)
    grads = lax.dot_general(weighted, out, NT, precision=lax.Precision.HIGHEST, preferred_element_type=F32)
    flat = [grads[i * E_DEV : (i + 1) * E_DEV] for i in range(ROWS)]
    goal = jnp.broadcast_to(goal_ref[...], (E_DEV, 128))
    goal = jnp.where(lax.broadcasted_iota(I32, (E_DEV, 128), 1) < 64, goal >> 4, goal & 15)
    p_ref[...] = jnp.concatenate(flat + [goal.astype(F32)], 1).astype(BF16)


def score_body(p0, p1, p2, p3, h_ref, keep_ref, send_ref, goal_ref, held):
    core, z = lax.axis_index("core"), lax.axis_index("z")
    for m, bits in enumerate((0, 4, 2, 6, 1, 5, 3, 7)):
        held[pl.ds(pl.multiple_of((z ^ bits) * C_DEV, C_DEV), C_DEV), :] = h_ref[m]
    ps = [p[...] for p in (p0, p1, p2, p3)]
    left = jnp.concatenate([p[:, :K_DEV] for p in ps], 0)
    score = lax.dot_general(left, held[...], NT, preferred_element_type=F32)
    first, second = score[:, :C_HALF], score[:, C_HALF:]
    keep_ref[...] = jnp.where(core == 0, first, second)
    send_ref[...] = jnp.where(core == 0, second, first)
    goal = jnp.concatenate([p[:, K_DEV:] for p in ps], 0).astype(F32)
    goal_ref[...] = jnp.broadcast_to(goal[:, :1] * 16.0 + goal[:, 64:65], (E_ALL, 128))


def total_body(a0, a1, a2, a3, goal_ref, flag_ref, s0, s1, s2, s3, slots_ref):
    core, y = lax.axis_index("core"), lax.axis_index("y")
    score = (a0[...] + a1[...]) + (a2[...] + a3[...])
    score = score * flag_ref[pl.ds(y * NC + core, 1), :]
    for d, ref in enumerate((s0, s1, s2, s3)):
        ref[...] = score[d * E_DEV : (d + 1) * E_DEV]
    first = ((y * NC + core) * C_HALF).astype(F32)
    goal = goal_ref[...] - first
    lane = lax.broadcasted_iota(I32, (E_ALL, 128), 1).astype(F32)
    sums = [
        jnp.sum(jnp.where(goal == lane + 128.0 * j, score[:, 128 * j : 128 * (j + 1)], 0.0), 0, keepdims=True)
        for j in range(C_HALF // 128)
    ]
    slots_ref[...] = jnp.zeros_like(slots_ref)
    for j in range(C_HALF // C_DEV):
        piece = sums[j // 2][:, (j % 2) * C_DEV : (j % 2 + 1) * C_DEV]
        slots_ref[pl.ds(core * (NZ // NC) + j, 1), 0, :] = piece


def join_body(s0, s1, s2, s3, slots_ref, out_ref):
    for d, ref in enumerate((s0, s1, s2, s3)):
        out_ref[d * E_DEV : (d + 1) * E_DEV] = ref[...]
    total = jnp.sum(slots_ref[...], 0)
    total = jnp.concatenate([total, jnp.zeros((1, C_HALF - C_DEV), F32)], 1)
    out_ref[E_ALL:] = jnp.broadcast_to(total, (8, C_HALF))


def lay_body(mine_ref, other_ref, out_ref, total_ref):
    core, y = lax.axis_index("core"), lax.axis_index("y")
    for d in range(NY):
        for part, ref in ((core, mine_ref), (1 - core, other_ref)):
            at = pl.multiple_of((y ^ d) * C_ALL + part * C_HALF, C_HALF)
            out_ref[:, pl.ds(at, C_HALF)] = ref[d * E_DEV : (d + 1) * E_DEV, :]
    total_ref[...] = mine_ref[E_ALL : E_ALL + 1, :C_DEV] + other_ref[E_ALL : E_ALL + 1, :C_DEV]


def per_device(
    down_matrix_feeds,
    result_slope_matrix,
    feed_sketch_factor,
    result_slope_factor,
    heldout_slope_entries,
    objective_of_sample,
    kept_choice_flags,
    token_sample_position,
):
    held = heldout_slope_entries[None]
    for bits in (4, 2, 1):
        held = jnp.concatenate([held, swap(held, "z", bits)], 0)

    keep, send = project(
        down_matrix_feeds, result_slope_matrix, feed_sketch_factor.T, result_slope_factor.T
    )
    sent = shaped(2 * ROWS + HALF, TOK, dtype=I16)
    low, half = shaped(ROWS, TOK), shaped(HALF, TOK)
    s1, s2, s3, in_own, out_chip = call(
        spread_body, [sent, sent, sent, low, half], keep, swap(send, "core", 1)
    )
    got = [swap(s, "x", d) for d, s in ((1, s1), (2, s2), (3, s3))]
    in_sum, out_half = call(add_body, [low, half], in_own, out_chip, *got)
    packed = call(
        outer_body,
        shaped(E_DEV, K_DEV + 128, dtype=BF16),
        in_sum,
        out_half,
        swap(out_half, "core", 1),
        token_sample_position,
        objective_of_sample[:, None],
    )
    packs = [packed] + [swap(packed, "y", d) for d in (1, 2, 3)]

    half = shaped(E_ALL, C_HALF)
    keep, send, goal = call(
        score_body,
        [half, half, shaped(E_ALL, 128)],
        *packs,
        held,
        scratch=[pltpu.VMEM((C_ALL, K_DEV), BF16)],
    )
    mine = keep + swap(send, "core", 1)
    flags = kept_choice_flags.astype(F32).reshape(NY * NC, C_HALF)
    piece = shaped(E_DEV, C_HALF)
    *pieces, slots = call(
        total_body,
        [piece] * NY + [shaped(NZ, 1, C_DEV)],
        mine,
        *[swap(mine, "x", d) for d in (1, 2, 3)],
        goal,
        flags,
    )
    back = [pieces[0]] + [swap(pieces[d], "y", d) for d in (1, 2, 3)]
    slots = lax.all_to_all(slots, "z", 0, 0, tiled=True)
    mine = call(join_body, shaped(E_ALL + 8, C_HALF), *back, slots)
    sample_affinity, totals = call(
        lay_body, [shaped(E_DEV, CHOICES), shaped(1, C_DEV)], mine, swap(mine, "core", 1)
    )
    return (sample_affinity, totals[0])


def solution(mesh):
    ex, tp = ("y", "z"), ("x", "core")
    chips = Mesh(mesh.devices.reshape(NY, NZ, NX, NC), ("y", "z", "x", "core"))
    placed = (
        P(ex, tp),
        P(ex, tp),
        P(tp, None),
        P(tp, None),
        P(ex, tp),
        P(ex),
        P(),
        P(ex, None),
    )
    return jax.shard_map(
        per_device, mesh=chips, in_specs=placed, out_specs=(P(ex, None), P(ex)), check_vma=False
    )
```

```python
import jax
import jax.numpy as jnp
from jax import lax
from jax.experimental import pallas as pl
from jax.experimental.pallas import tpu as pltpu
from jax.sharding import Mesh
from jax.sharding import PartitionSpec as P

NY, NZ, NX, NC = 4, 8, 4, 2
SIZES = dict(y=NY, z=NZ, x=NX, core=NC)
RANK, TOK, E_DEV, C_DEV, K_DEV, CHOICES = 64, 1024, 16, 64, 512, 2048
ROWS = RANK // (NX * NC)
HALF = RANK // 2
E_ALL, C_ALL = NY * E_DEV, NZ * C_DEV
C_HALF = C_ALL // NC
F32, BF16, I32, I16 = jnp.float32, jnp.bfloat16, jnp.int32, jnp.int16
NT = (((1,), (1,)), ((), ()))
CHUNK = 512
VMEM_LIMIT = 48 * 1024 * 1024


def swap(value, axis, bits):
    return lax.ppermute(value, axis, [(i, i ^ bits) for i in range(SIZES[axis])])


def shaped(*dims, dtype=F32):
    return jax.ShapeDtypeStruct(dims, dtype)


def call(body, outs, *args, scratch=(), after=None, work=0):
    count = len(args)
    specs = [pl.BlockSpec(memory_space=pltpu.VMEM)] * count
    run = body
    if after is not None:
        run = lambda *refs: body(*refs[:count], *refs[count + 1 :])
        specs, args = specs + [pl.BlockSpec(memory_space=pl.ANY)], args + (after,)
    return pl.pallas_call(
        run,
        out_shape=outs,
        in_specs=specs,
        scratch_shapes=scratch,
        compiler_params=pltpu.CompilerParams(vmem_limit_bytes=VMEM_LIMIT),
        cost_estimate=pl.CostEstimate(flops=work, transcendentals=0, bytes_accessed=work // 100) if work else None,
    )(*args)


def project_body(
    x_hbm, y_hbm, w_in_hbm, w_out_hbm, h_hbm, keep_ref, send_ref, h_ref, parts, w_in, w_out, low, out, sems
):
    core = lax.axis_index("core")
    steps = [(y_hbm, w_out, out, k) for k in range(y_hbm.shape[1] // CHUNK)]
    steps += [(x_hbm, w_in, low, k) for k in range(x_hbm.shape[1] // CHUNK)]
    copies = [
        pltpu.make_async_copy(src.at[:, pl.ds(k * CHUNK, CHUNK)], parts.at[n], sems.at[n])
        for n, (src, _, _, k) in enumerate(steps)
    ]
    copy_out = pltpu.make_async_copy(w_out_hbm, w_out, sems.at[len(steps)])
    copy_in = pltpu.make_async_copy(w_in_hbm, w_in, sems.at[len(steps) + 1])
    copy_out.start()
    copies[0].start()
    copy_in.start()
    for copy in copies[1:]:
        copy.start()
    copy_held = pltpu.make_async_copy(h_hbm, h_ref, sems.at[len(steps) + 2])
    copy_held.start()
    copy_out.wait()
    for n, (src, weights, total, k) in enumerate(steps):
        copies[n].wait()
        if src is x_hbm and k == 0:
            copy_in.wait()
        part = lax.dot_general(
            weights[:, k * CHUNK : (k + 1) * CHUNK], parts[n], NT, preferred_element_type=F32
        )
        if k == 0:
            total[...] = part
        else:
            total[...] += part
    copy_held.wait()
    for c in range(NC):
        part = [low[(NC * j + c) * ROWS : (NC * j + c + 1) * ROWS] for j in range(NX)]
        part = jnp.concatenate(part + [out[c * HALF : (c + 1) * HALF]], 0)

        @pl.when(core == c)
        def _():
            keep_ref[...] = part

        @pl.when(core != c)
        def _():
            send_ref[...] = part


def project(x, y, w_in, w_out, held):
    steps = (x.shape[1] + y.shape[1]) // CHUNK
    args = [pltpu.with_memory_space_constraint(a, pltpu.HBM) for a in (x, y, w_in, w_out, held)]
    return pl.pallas_call(
        project_body,
        in_specs=[pl.BlockSpec(memory_space=pltpu.HBM)] * 5,
        out_shape=[shaped(RANK, TOK), shaped(RANK, TOK), shaped(*held.shape, dtype=BF16)],
        scratch_shapes=[
            pltpu.VMEM((steps, TOK, CHUNK), BF16),
            pltpu.VMEM(w_in.shape, BF16),
            pltpu.VMEM(w_out.shape, BF16),
            pltpu.VMEM((RANK, TOK), F32),
            pltpu.VMEM((RANK, TOK), F32),
            pltpu.SemaphoreType.DMA((steps + 3,)),
        ],
        compiler_params=pltpu.CompilerParams(vmem_limit_bytes=VMEM_LIMIT),
        cost_estimate=pl.CostEstimate(
            flops=2 * RANK * x.size + 2 * RANK * y.size, transcendentals=0, bytes_accessed=2 * (x.size + y.size)
        ),
    )(*args)


def coded(value):
    top = jnp.maximum(jnp.max(jnp.abs(value), 0, keepdims=True), 1e-30)
    power = jnp.clip(jnp.floor(jnp.log2(top)) - 13.0, -100.0, 100.0)
    return jnp.round(value / jnp.exp2(power)), power


def spread_body(keep_ref, got_ref, s1_ref, s2_ref, s3_ref, in_ref, out_ref):
    x = lax.axis_index("x")
    out = keep_ref[NX * ROWS :] + got_ref[NX * ROWS :]
    out_ref[...] = out
    out_code, out_power = coded(out)
    line = lax.broadcasted_iota(I32, (ROWS, TOK), 0)
    for d, ref in ((1, s1_ref), (2, s2_ref), (3, s3_ref), (0, None)):
        at = pl.ds(pl.multiple_of((x ^ d) * ROWS, ROWS), ROWS)
        part = keep_ref[at, :] + got_ref[at, :]
        if ref is None:
            in_ref[...] = part
        else:
            code, power = coded(part)
            powers = jnp.where(line == 0, power, out_power)
            ref[...] = jnp.concatenate([code, out_code, powers], 0).astype(I32).astype(I16)


def join_body(first_ref, second_ref, out_ref):
    out_ref[: first_ref.shape[0]] = first_ref[...]
    out_ref[first_ref.shape[0] :] = second_ref[...]


def add_body(in_ref, out_ref, g1_ref, g2_ref, g3_ref, low_ref, half_ref):
    low, half = in_ref[...], out_ref[...]
    for ref in (g1_ref, g2_ref, g3_ref):
        got = ref[...].astype(I32).astype(F32)
        powers = jnp.exp2(got[ROWS + HALF :])
        low = low + got[:ROWS] * powers[:1]
        half = half + got[ROWS : ROWS + HALF] * powers[1:2]
    low_ref[...] = low
    half_ref[...] = half


def parts_of(value):
    high = value.astype(BF16)
    return high, (value - high.astype(F32)).astype(BF16)


def outer_body(in_ref, mine_ref, other_ref, where_ref, goal_ref, p_ref):
    core = lax.axis_index("core")
    low, mine, other = in_ref[...], mine_ref[...], other_ref[...]
    out = jnp.concatenate([jnp.where(core == 0, mine, other), jnp.where(core == 0, other, mine)], 0)
    out_high, out_low = parts_of(out)
    onehot = lax.broadcasted_iota(I32, (E_DEV, TOK), 0) == where_ref[...]
    pairs = [parts_of(jnp.where(onehot, low[i : i + 1], 0.0)) for i in range(ROWS)]
    high = jnp.concatenate([p[0] for p in pairs], 0)
    rest = jnp.concatenate([p[1] for p in pairs], 0)
    dot = lambda u, v: lax.dot_general(u, v, NT, preferred_element_type=F32)
    grads = dot(high, out_high) + (dot(high, out_low) + dot(rest, out_high))
    flat = [grads[i * E_DEV : (i + 1) * E_DEV] for i in range(ROWS)]
    goal = jnp.broadcast_to(goal_ref[...], (E_DEV, 128))
    goal = jnp.where(lax.broadcasted_iota(I32, (E_DEV, 128), 1) < 64, goal >> 4, goal & 15)
    p_ref[...] = jnp.concatenate(flat + [goal.astype(F32)], 1).astype(BF16)


def score_body(p0, p1, p2, p3, first_ref, second_ref, keep_ref, send_ref, goal_ref, held):
    core, z = lax.axis_index("core"), lax.axis_index("z")
    for m, bits in enumerate((0, 4, 2, 6, 1, 5, 3, 7)):
        at = pl.ds(pl.multiple_of((z ^ bits) * C_DEV, C_DEV), C_DEV)
        held[at, :] = (first_ref, second_ref)[m // (NZ // 2)][m % (NZ // 2)]
    ps = [p[...] for p in (p0, p1, p2, p3)]
    left = jnp.concatenate([p[:, :K_DEV] for p in ps], 0)
    score = lax.dot_general(left, held[...], NT, preferred_element_type=F32)
    first, second = score[:, :C_HALF], score[:, C_HALF:]
    keep_ref[...] = jnp.where(core == 0, first, second)
    send_ref[...] = jnp.where(core == 0, second, first)
    goal = jnp.concatenate([p[:, K_DEV:] for p in ps], 0).astype(F32)
    goal_ref[...] = jnp.broadcast_to(goal[:, :1] * 16.0 + goal[:, 64:65], (E_ALL, 128))


def total_body(a0, a1, a2, a3, goal_ref, s0, s1, s2, s3, slots_ref):
    core, y = lax.axis_index("core"), lax.axis_index("y")
    score = (a0[...] + a1[...]) + (a2[...] + a3[...])
    for d, ref in enumerate((s0, s1, s2, s3)):
        ref[...] = score[d * E_DEV : (d + 1) * E_DEV]
    first = ((y * NC + core) * C_HALF).astype(F32)
    goal = goal_ref[...] - first
    lane = lax.broadcasted_iota(I32, (E_ALL, 128), 1).astype(F32)
    slots_ref[...] = jnp.zeros_like(slots_ref)
    for j in range(C_HALF // 128):
        hit = goal == lane + 128.0 * j
        sums = jnp.sum(jnp.where(hit, score[:, 128 * j : 128 * (j + 1)], 0.0), 0, keepdims=True)
        for i in range(128 // C_DEV):
            piece = sums[:, i * C_DEV : (i + 1) * C_DEV]
            at = (core * (NZ // NC) + j * (128 // C_DEV) + i) * NC
            for c in range(NC):
                slots_ref[pl.ds(at + c, 1), 0, :] = piece


def lay_body(mine_ref, other_ref, flag_ref, own_flag_ref, slots_ref, out_ref, total_ref):
    core, y, z = (lax.axis_index(name) for name in ("core", "y", "z"))
    for d in range(NY):
        for part, ref in ((core, mine_ref), (1 - core, other_ref)):
            at = pl.ds(pl.multiple_of((y ^ d) * C_ALL + part * C_HALF, C_HALF), C_HALF)
            out_ref[:, at] = ref[d * E_DEV : (d + 1) * E_DEV, :] * flag_ref[:, at].astype(F32)
    flags = own_flag_ref[pl.ds(y * NZ + z, 1), :].astype(F32)
    total_ref[...] = jnp.sum(slots_ref[...], 0) * flags


def per_device(
    down_matrix_feeds,
    result_slope_matrix,
    feed_sketch_factor,
    result_slope_factor,
    heldout_slope_entries,
    objective_of_sample,
    kept_choice_flags,
    token_sample_position,
):
    far = swap(heldout_slope_entries[None], "z", 4)
    keep, away, held = project(
        down_matrix_feeds,
        result_slope_matrix,
        feed_sketch_factor.T,
        result_slope_factor.T,
        heldout_slope_entries,
    )
    held = jnp.concatenate([held[None], far], 0)
    far = swap(held, "z", 2)

    sent = shaped(2 * ROWS + HALF, TOK, dtype=I16)
    low, half = shaped(ROWS, TOK), shaped(HALF, TOK)
    s1, s2, s3, in_own, out_chip = call(
        spread_body, [sent, sent, sent, low, half], keep, swap(away, "core", 1)
    )
    got = {d: swap(s, "x", d) for d, s in ((2, s2), (1, s1), (3, s3))}
    held = call(join_body, shaped(4, C_DEV, K_DEV, dtype=BF16), held, far, after=in_own)
    far = swap(held, "z", 1)
    in_sum, out_half = call(add_body, [low, half], in_own, out_chip, got[1], got[2], got[3])
    packed = call(
        outer_body,
        shaped(E_DEV, K_DEV + 128, dtype=BF16),
        in_sum,
        out_half,
        swap(out_half, "core", 1),
        token_sample_position,
        objective_of_sample[:, None],
        work=400000000,
    )
    packs = {d: swap(packed, "y", d) for d in (2, 1, 3)}

    side = shaped(E_ALL, C_HALF)
    keep, send, goal = call(
        score_body,
        [side, side, shaped(E_ALL, 128)],
        packed,
        packs[1],
        packs[2],
        packs[3],
        held,
        far,
        scratch=[pltpu.VMEM((C_ALL, K_DEV), BF16)],
    )
    score = keep + swap(send, "core", 1)
    got = {d: swap(score, "x", d) for d in (2, 1, 3)}
    piece = shaped(E_DEV, C_HALF)
    *pieces, slots = call(
        total_body,
        [piece] * NY + [shaped(NZ * NC, 1, C_DEV)],
        score,
        got[1],
        got[2],
        got[3],
        goal,
    )
    got = {d: swap(pieces[d], "y", d) for d in (2, 1, 3)}
    mine, slots = lax.optimization_barrier(
        (jnp.concatenate([pieces[0], got[1], got[2], got[3]], 0), slots)
    )
    sample_affinity, totals = call(
        lay_body,
        [shaped(E_DEV, CHOICES), shaped(1, C_DEV)],
        mine,
        swap(mine, "core", 1),
        kept_choice_flags.reshape(1, CHOICES),
        kept_choice_flags.reshape(NY * NZ, C_DEV),
        lax.all_to_all(slots, ("z", "core"), 0, 0, tiled=True),
    )
    return (sample_affinity, totals[0])


def solution(mesh):
    ex, tp = ("y", "z"), ("x", "core")
    chips = Mesh(mesh.devices.reshape(NY, NZ, NX, NC), ("y", "z", "x", "core"))
    placed = (
        P(ex, tp),
        P(ex, tp),
        P(tp, None),
        P(tp, None),
        P(ex, tp),
        P(ex),
        P(),
        P(ex, None),
    )
    return jax.shard_map(
        per_device, mesh=chips, in_specs=placed, out_specs=(P(ex, None), P(ex)), check_vma=False
    )
```

```python
import jax
import jax.numpy as jnp
from jax import lax
from jax.experimental import pallas as pl
from jax.experimental.pallas import tpu as pltpu
from jax.sharding import Mesh
from jax.sharding import PartitionSpec as P

NY, NZ, NX, NC = 4, 8, 4, 2
SIZES = dict(y=NY, z=NZ, x=NX, core=NC)
RANK, TOK, E_DEV, C_DEV, K_DEV, CHOICES = 64, 1024, 16, 64, 512, 2048
ROWS = RANK // (NX * NC)
HALF = RANK // 2
E_ALL, C_ALL = NY * E_DEV, NZ * C_DEV
C_HALF = C_ALL // NC
F32, BF16, I32, I16 = jnp.float32, jnp.bfloat16, jnp.int32, jnp.int16
NT = (((1,), (1,)), ((), ()))
CHUNK = 512
VMEM_LIMIT = 48 * 1024 * 1024


def swap(value, axis, bits):
    return lax.ppermute(value, axis, [(i, i ^ bits) for i in range(SIZES[axis])])


def shaped(*dims, dtype=F32):
    return jax.ShapeDtypeStruct(dims, dtype)


def call(body, outs, *args, scratch=(), after=None, work=0):
    count = len(args)
    specs = [pl.BlockSpec(memory_space=pltpu.VMEM)] * count
    run = body
    if after is not None:
        run = lambda *refs: body(*refs[:count], *refs[count + 1 :])
        specs, args = specs + [pl.BlockSpec(memory_space=pl.ANY)], args + (after,)
    return pl.pallas_call(
        run,
        out_shape=outs,
        in_specs=specs,
        scratch_shapes=scratch,
        compiler_params=pltpu.CompilerParams(vmem_limit_bytes=VMEM_LIMIT),
        cost_estimate=pl.CostEstimate(flops=work, transcendentals=0, bytes_accessed=work // 100) if work else None,
    )(*args)


def project_body(
    x_hbm, y_hbm, w_in_hbm, w_out_hbm, h_hbm, keep_ref, send_ref, h_ref, parts, w_in, w_out, low, out, sems
):
    core = lax.axis_index("core")
    steps = [(y_hbm, w_out, out, k) for k in range(y_hbm.shape[1] // CHUNK)]
    steps += [(x_hbm, w_in, low, k) for k in range(x_hbm.shape[1] // CHUNK)]
    copies = [
        pltpu.make_async_copy(src.at[:, pl.ds(k * CHUNK, CHUNK)], parts.at[n], sems.at[n])
        for n, (src, _, _, k) in enumerate(steps)
    ]
    copy_out = pltpu.make_async_copy(w_out_hbm, w_out, sems.at[len(steps)])
    copy_in = pltpu.make_async_copy(w_in_hbm, w_in, sems.at[len(steps) + 1])
    copy_out.start()
    copies[0].start()
    copy_in.start()
    for copy in copies[1:]:
        copy.start()
    copy_held = pltpu.make_async_copy(h_hbm, h_ref, sems.at[len(steps) + 2])
    copy_held.start()
    copy_out.wait()
    for n, (src, weights, total, k) in enumerate(steps):
        copies[n].wait()
        if src is x_hbm and k == 0:
            copy_in.wait()
        part = lax.dot_general(
            weights[:, k * CHUNK : (k + 1) * CHUNK], parts[n], NT, preferred_element_type=F32
        )
        if k == 0:
            total[...] = part
        else:
            total[...] += part
    copy_held.wait()
    for c in range(NC):
        part = [low[(NC * j + c) * ROWS : (NC * j + c + 1) * ROWS] for j in range(NX)]
        part = jnp.concatenate(part + [out[c * HALF : (c + 1) * HALF]], 0)

        @pl.when(core == c)
        def _():
            keep_ref[...] = part

        @pl.when(core != c)
        def _():
            send_ref[...] = part


def project(x, y, w_in, w_out, held):
    steps = (x.shape[1] + y.shape[1]) // CHUNK
    args = [pltpu.with_memory_space_constraint(a, pltpu.HBM) for a in (x, y, w_in, w_out, held)]
    return pl.pallas_call(
        project_body,
        in_specs=[pl.BlockSpec(memory_space=pltpu.HBM)] * 5,
        out_shape=[shaped(RANK, TOK), shaped(RANK, TOK), shaped(*held.shape, dtype=BF16)],
        scratch_shapes=[
            pltpu.VMEM((steps, TOK, CHUNK), BF16),
            pltpu.VMEM(w_in.shape, BF16),
            pltpu.VMEM(w_out.shape, BF16),
            pltpu.VMEM((RANK, TOK), F32),
            pltpu.VMEM((RANK, TOK), F32),
            pltpu.SemaphoreType.DMA((steps + 3,)),
        ],
        compiler_params=pltpu.CompilerParams(vmem_limit_bytes=VMEM_LIMIT),
        cost_estimate=pl.CostEstimate(
            flops=2 * RANK * x.size + 2 * RANK * y.size, transcendentals=0, bytes_accessed=2 * (x.size + y.size)
        ),
    )(*args)


def coded(value):
    top = jnp.maximum(jnp.max(jnp.abs(value), 0, keepdims=True), 1e-30)
    power = jnp.clip(jnp.floor(jnp.log2(top)) - 13.0, -100.0, 100.0)
    return jnp.round(value / jnp.exp2(power)), power


def spread_body(keep_ref, got_ref, s1_ref, s2_ref, s3_ref, in_ref, out_ref):
    x = lax.axis_index("x")
    out = keep_ref[NX * ROWS :] + got_ref[NX * ROWS :]
    out_ref[...] = out
    out_code, out_power = coded(out)
    line = lax.broadcasted_iota(I32, (ROWS, TOK), 0)
    for d, ref in ((1, s1_ref), (2, s2_ref), (3, s3_ref), (0, None)):
        at = pl.ds(pl.multiple_of((x ^ d) * ROWS, ROWS), ROWS)
        part = keep_ref[at, :] + got_ref[at, :]
        if ref is None:
            in_ref[...] = part
        else:
            code, power = coded(part)
            powers = jnp.where(line == 0, power, out_power)
            ref[...] = jnp.concatenate([code, out_code, powers], 0).astype(I32).astype(I16)


def join_body(first_ref, second_ref, out_ref):
    out_ref[: first_ref.shape[0]] = first_ref[...]
    out_ref[first_ref.shape[0] :] = second_ref[...]


def add_body(in_ref, out_ref, g1_ref, g2_ref, g3_ref, low_ref, half_ref):
    low, half = in_ref[...], out_ref[...]
    for ref in (g1_ref, g2_ref, g3_ref):
        got = ref[...].astype(I32).astype(F32)
        powers = jnp.exp2(got[ROWS + HALF :])
        low = low + got[:ROWS] * powers[:1]
        half = half + got[ROWS : ROWS + HALF] * powers[1:2]
    low_ref[...] = low
    half_ref[...] = half


def parts_of(value):
    high = value.astype(BF16)
    return high, (value - high.astype(F32)).astype(BF16)


def outer_body(in_ref, mine_ref, other_ref, where_ref, goal_ref, p_ref):
    core = lax.axis_index("core")
    low, mine, other = in_ref[...], mine_ref[...], other_ref[...]
    out = jnp.concatenate([jnp.where(core == 0, mine, other), jnp.where(core == 0, other, mine)], 0)
    out_high, out_low = parts_of(out)
    onehot = lax.broadcasted_iota(I32, (E_DEV, TOK), 0) == where_ref[...]
    pairs = [parts_of(jnp.where(onehot, low[i : i + 1], 0.0)) for i in range(ROWS)]
    high = jnp.concatenate([p[0] for p in pairs], 0)
    rest = jnp.concatenate([p[1] for p in pairs], 0)
    dot = lambda u, v: lax.dot_general(u, v, NT, preferred_element_type=F32)
    grads = dot(high, out_high) + (dot(high, out_low) + dot(rest, out_high))
    flat = [grads[i * E_DEV : (i + 1) * E_DEV] for i in range(ROWS)]
    goal = jnp.broadcast_to(goal_ref[...], (E_DEV, 128))
    goal = jnp.where(lax.broadcasted_iota(I32, (E_DEV, 128), 1) < 64, goal >> 4, goal & 15)
    p_ref[...] = jnp.concatenate(flat + [goal.astype(F32)], 1).astype(BF16)


def score_body(p0, p1, p2, p3, first_ref, second_ref, keep_ref, send_ref, goal_ref, held):
    core, z = lax.axis_index("core"), lax.axis_index("z")
    for m, bits in enumerate((0, 2, 4, 6, 1, 3, 5, 7)):
        at = pl.ds(pl.multiple_of((z ^ bits) * C_DEV, C_DEV), C_DEV)
        held[at, :] = (first_ref, second_ref)[m // (NZ // 2)][m % (NZ // 2)]
    ps = [p[...] for p in (p0, p1, p2, p3)]
    left = jnp.concatenate([p[:, :K_DEV] for p in ps], 0)
    score = lax.dot_general(left, held[...], NT, preferred_element_type=F32)
    first, second = score[:, :C_HALF], score[:, C_HALF:]
    keep_ref[...] = jnp.where(core == 0, first, second)
    send_ref[...] = jnp.where(core == 0, second, first)
    goal = jnp.concatenate([p[:, K_DEV:] for p in ps], 0).astype(F32)
    goal_ref[...] = jnp.broadcast_to(goal[:, :1] * 16.0 + goal[:, 64:65], (E_ALL, 128))


def total_body(a0, a1, a2, a3, goal_ref, s0, s1, s2, s3, slots_ref):
    core, y = lax.axis_index("core"), lax.axis_index("y")
    score = (a0[...] + a1[...]) + (a2[...] + a3[...])
    for d, ref in enumerate((s0, s1, s2, s3)):
        ref[...] = score[d * E_DEV : (d + 1) * E_DEV]
    first = ((y * NC + core) * C_HALF).astype(F32)
    goal = goal_ref[...] - first
    lane = lax.broadcasted_iota(I32, (E_ALL, 128), 1).astype(F32)
    pieces = []
    for j in range(C_HALF // 128):
        hit = goal == lane + 128.0 * j
        sums = jnp.sum(jnp.where(hit, score[:, 128 * j : 128 * (j + 1)], 0.0), 0, keepdims=True)
        pieces += [sums[:, i * C_DEV : (i + 1) * C_DEV] for i in range(128 // C_DEV) for _ in range(NC)]
    rows = jnp.concatenate(pieces, 0)
    for c in range(NC):
        slots_ref[c * len(pieces) : (c + 1) * len(pieces)] = jnp.where(core == c, rows, 0.0)


def lay_body(mine_ref, other_ref, flag_ref, own_flag_ref, slots_ref, out_ref, total_ref):
    core, y, z = (lax.axis_index(name) for name in ("core", "y", "z"))
    for d in range(NY):
        for part, ref in ((core, mine_ref), (1 - core, other_ref)):
            at = pl.ds(pl.multiple_of((y ^ d) * C_ALL + part * C_HALF, C_HALF), C_HALF)
            out_ref[:, at] = ref[d * E_DEV : (d + 1) * E_DEV, :] * flag_ref[:, at].astype(F32)
    flags = own_flag_ref[pl.ds(y * NZ + z, 1), :].astype(F32)
    total_ref[...] = jnp.sum(slots_ref[...], 0, keepdims=True) * flags


def per_device(
    down_matrix_feeds,
    result_slope_matrix,
    feed_sketch_factor,
    result_slope_factor,
    heldout_slope_entries,
    objective_of_sample,
    kept_choice_flags,
    token_sample_position,
):
    far = swap(heldout_slope_entries[None], "z", 2)
    keep, away, held = project(
        down_matrix_feeds,
        result_slope_matrix,
        feed_sketch_factor.T,
        result_slope_factor.T,
        heldout_slope_entries,
    )
    held = jnp.concatenate([held[None], far], 0)
    far = swap(held, "z", 4)

    sent = shaped(2 * ROWS + HALF, TOK, dtype=I16)
    low, half = shaped(ROWS, TOK), shaped(HALF, TOK)
    s1, s2, s3, in_own, out_chip = call(
        spread_body, [sent, sent, sent, low, half], keep, swap(away, "core", 1)
    )
    got = {d: swap(s, "x", d) for d, s in ((2, s2), (1, s1), (3, s3))}
    held = call(join_body, shaped(NZ // 2, C_DEV, K_DEV, dtype=BF16), held, far, after=in_own)
    far = swap(held, "z", 1)
    in_sum, out_half = call(add_body, [low, half], in_own, out_chip, got[1], got[2], got[3])
    packed = call(
        outer_body,
        shaped(E_DEV, K_DEV + 128, dtype=BF16),
        in_sum,
        out_half,
        swap(out_half, "core", 1),
        token_sample_position,
        objective_of_sample[:, None],
        work=400_000_000,
    )
    packs = {d: swap(packed, "y", d) for d in (2, 1, 3)}

    side = shaped(E_ALL, C_HALF)
    keep, send, goal = call(
        score_body,
        [side, side, shaped(E_ALL, 128)],
        packed,
        packs[1],
        packs[2],
        packs[3],
        held,
        far,
        scratch=[pltpu.VMEM((C_ALL, K_DEV), BF16)],
    )
    score = keep + swap(send, "core", 1)
    got = {d: swap(score, "x", d) for d in (2, 1, 3)}
    piece = shaped(E_DEV, C_HALF)
    *pieces, slots = call(
        total_body,
        [piece] * NY + [shaped(NZ * NC, C_DEV)],
        score,
        got[1],
        got[2],
        got[3],
        goal,
    )
    got = {d: swap(pieces[d], "y", d) for d in (2, 1, 3)}
    mine = jnp.concatenate([pieces[0], got[1], got[2], got[3]], 0)
    sample_affinity, totals = call(
        lay_body,
        [shaped(E_DEV, CHOICES), shaped(1, C_DEV)],
        mine,
        swap(mine, "core", 1),
        kept_choice_flags.reshape(1, CHOICES),
        kept_choice_flags.reshape(NY * NZ, C_DEV),
        lax.all_to_all(slots, ("z", "core"), 0, 0, tiled=True),
    )
    return (sample_affinity, totals[0])


def solution(mesh):
    ex, tp = ("y", "z"), ("x", "core")
    chips = Mesh(mesh.devices.reshape(NY, NZ, NX, NC), ("y", "z", "x", "core"))
    placed = (
        P(ex, tp),
        P(ex, tp),
        P(tp, None),
        P(tp, None),
        P(ex, tp),
        P(ex),
        P(),
        P(ex, None),
    )
    return jax.shard_map(
        per_device, mesh=chips, in_specs=placed, out_specs=(P(ex, None), P(ex)), check_vma=False
    )
```

```python
import jax
import jax.numpy as jnp
from jax import lax
from jax.experimental import pallas as pl
from jax.experimental.pallas import tpu as pltpu
from jax.sharding import Mesh
from jax.sharding import PartitionSpec as P

NY, NZ, NX, NC = 4, 8, 4, 2
SIZES = dict(y=NY, z=NZ, x=NX, core=NC)
RANK, TOK, E_DEV, C_DEV, K_DEV, CHOICES = 64, 1024, 16, 64, 512, 2048
ROWS = RANK // (NX * NC)
HALF = RANK // 2
E_ALL, C_ALL = NY * E_DEV, NZ * C_DEV
C_HALF = C_ALL // NC
F32, BF16, I32, I16 = jnp.float32, jnp.bfloat16, jnp.int32, jnp.int16
NT = (((1,), (1,)), ((), ()))
CHUNK = 512
VMEM_LIMIT = 48 * 1024 * 1024


def swap(value, axis, bits):
    return lax.ppermute(value, axis, [(i, i ^ bits) for i in range(SIZES[axis])])


def shaped(*dims, dtype=F32):
    return jax.ShapeDtypeStruct(dims, dtype)


def call(body, outs, *args, scratch=(), after=None, work=0):
    count = len(args)
    specs = [pl.BlockSpec(memory_space=pltpu.VMEM)] * count
    run = body
    if after is not None:
        run = lambda *refs: body(*refs[:count], *refs[count + 1 :])
        specs, args = specs + [pl.BlockSpec(memory_space=pl.ANY)], args + (after,)
    return pl.pallas_call(
        run,
        out_shape=outs,
        in_specs=specs,
        scratch_shapes=scratch,
        compiler_params=pltpu.CompilerParams(vmem_limit_bytes=VMEM_LIMIT),
        cost_estimate=pl.CostEstimate(flops=work, transcendentals=0, bytes_accessed=work // 100) if work else None,
    )(*args)


def project_body(
    x_hbm, y_hbm, w_in_hbm, w_out_hbm, h_hbm, keep_ref, send_ref, h_ref, parts, w_in, w_out, low, out, sems
):
    core = lax.axis_index("core")
    steps = [(y_hbm, w_out, out, k) for k in range(y_hbm.shape[1] // CHUNK)]
    steps += [(x_hbm, w_in, low, k) for k in range(x_hbm.shape[1] // CHUNK)]
    copies = [
        pltpu.make_async_copy(src.at[:, pl.ds(k * CHUNK, CHUNK)], parts.at[n], sems.at[n])
        for n, (src, _, _, k) in enumerate(steps)
    ]
    copy_out = pltpu.make_async_copy(w_out_hbm, w_out, sems.at[len(steps)])
    copy_in = pltpu.make_async_copy(w_in_hbm, w_in, sems.at[len(steps) + 1])
    copy_out.start()
    copies[0].start()
    copy_in.start()
    for copy in copies[1:]:
        copy.start()
    copy_held = pltpu.make_async_copy(h_hbm, h_ref, sems.at[len(steps) + 2])
    copy_held.start()
    copy_out.wait()
    for n, (src, weights, total, k) in enumerate(steps):
        copies[n].wait()
        if src is x_hbm and k == 0:
            copy_in.wait()
        part = lax.dot_general(
            weights[:, k * CHUNK : (k + 1) * CHUNK], parts[n], NT, preferred_element_type=F32
        )
        if k == 0:
            total[...] = part
        else:
            total[...] += part
    copy_held.wait()
    for c in range(NC):
        part = [low[(NC * j + c) * ROWS : (NC * j + c + 1) * ROWS] for j in range(NX)]
        part = jnp.concatenate(part + [out[c * HALF : (c + 1) * HALF]], 0)

        @pl.when(core == c)
        def _():
            keep_ref[...] = part

        @pl.when(core != c)
        def _():
            send_ref[...] = part


def project(x, y, w_in, w_out, held):
    steps = (x.shape[1] + y.shape[1]) // CHUNK
    args = [pltpu.with_memory_space_constraint(a, pltpu.HBM) for a in (x, y, w_in, w_out, held)]
    return pl.pallas_call(
        project_body,
        in_specs=[pl.BlockSpec(memory_space=pltpu.HBM)] * 5,
        out_shape=[shaped(RANK, TOK), shaped(RANK, TOK), shaped(*held.shape, dtype=BF16)],
        scratch_shapes=[
            pltpu.VMEM((steps, TOK, CHUNK), BF16),
            pltpu.VMEM(w_in.shape, BF16),
            pltpu.VMEM(w_out.shape, BF16),
            pltpu.VMEM((RANK, TOK), F32),
            pltpu.VMEM((RANK, TOK), F32),
            pltpu.SemaphoreType.DMA((steps + 3,)),
        ],
        compiler_params=pltpu.CompilerParams(vmem_limit_bytes=VMEM_LIMIT),
        cost_estimate=pl.CostEstimate(
            flops=2 * RANK * x.size + 2 * RANK * y.size, transcendentals=0, bytes_accessed=2 * (x.size + y.size)
        ),
    )(*args)


def coded(value):
    top = jnp.maximum(jnp.max(jnp.abs(value), 0, keepdims=True), 1e-30)
    power = jnp.clip(jnp.floor(jnp.log2(top)) - 13.0, -100.0, 100.0)
    return jnp.round(value / jnp.exp2(power)), power


def spread_body(keep_ref, got_ref, s1_ref, s2_ref, s3_ref, in_ref, out_ref):
    x = lax.axis_index("x")
    out = keep_ref[NX * ROWS :] + got_ref[NX * ROWS :]
    out_ref[...] = out
    out_code, out_power = coded(out)
    line = lax.broadcasted_iota(I32, (ROWS, TOK), 0)
    for d, ref in ((1, s1_ref), (2, s2_ref), (3, s3_ref), (0, None)):
        at = pl.ds(pl.multiple_of((x ^ d) * ROWS, ROWS), ROWS)
        part = keep_ref[at, :] + got_ref[at, :]
        if ref is None:
            in_ref[...] = part
        else:
            code, power = coded(part)
            powers = jnp.where(line == 0, power, out_power)
            ref[...] = jnp.concatenate([code, out_code, powers], 0).astype(I32).astype(I16)


def join_body(first_ref, second_ref, out_ref):
    out_ref[: first_ref.shape[0]] = first_ref[...]
    out_ref[first_ref.shape[0] :] = second_ref[...]


def add_body(in_ref, out_ref, g1_ref, g2_ref, g3_ref, low_ref, half_ref):
    low, half = in_ref[...], out_ref[...]
    for ref in (g1_ref, g2_ref, g3_ref):
        got = ref[...].astype(I32).astype(F32)
        powers = jnp.exp2(got[ROWS + HALF :])
        low = low + got[:ROWS] * powers[:1]
        half = half + got[ROWS : ROWS + HALF] * powers[1:2]
    low_ref[...] = low
    half_ref[...] = half


def parts_of(value):
    high = value.astype(BF16)
    return high, (value - high.astype(F32)).astype(BF16)


def outer_body(in_ref, mine_ref, other_ref, where_ref, goal_ref, p_ref):
    core = lax.axis_index("core")
    low, mine, other = in_ref[...], mine_ref[...], other_ref[...]
    out = jnp.concatenate([jnp.where(core == 0, mine, other), jnp.where(core == 0, other, mine)], 0)
    out_high, out_low = parts_of(out)
    onehot = lax.broadcasted_iota(I32, (E_DEV, TOK), 0) == where_ref[...]
    pairs = [parts_of(jnp.where(onehot, low[i : i + 1], 0.0)) for i in range(ROWS)]
    high = jnp.concatenate([p[0] for p in pairs], 0)
    rest = jnp.concatenate([p[1] for p in pairs], 0)
    dot = lambda u, v: lax.dot_general(u, v, NT, preferred_element_type=F32)
    grads = dot(high, out_high) + (dot(high, out_low) + dot(rest, out_high))
    flat = [grads[i * E_DEV : (i + 1) * E_DEV] for i in range(ROWS)]
    goal = jnp.broadcast_to(goal_ref[...], (E_DEV, 128))
    goal = jnp.where(lax.broadcasted_iota(I32, (E_DEV, 128), 1) < 64, goal >> 4, goal & 15)
    p_ref[...] = jnp.concatenate(flat + [goal.astype(F32)], 1).astype(BF16)


def score_body(p0, p1, p2, p3, first_ref, second_ref, keep_ref, send_ref, goal_ref, held):
    core, z = lax.axis_index("core"), lax.axis_index("z")
    for m, bits in enumerate((0, 7, 2, 5, 1, 6, 3, 4)):
        at = pl.ds(pl.multiple_of((z ^ bits) * C_DEV, C_DEV), C_DEV)
        held[at, :] = (first_ref, second_ref)[m // (NZ // 2)][m % (NZ // 2)]
    ps = [p[...] for p in (p0, p1, p2, p3)]
    left = jnp.concatenate([p[:, :K_DEV] for p in ps], 0)
    score = lax.dot_general(left, held[...], NT, preferred_element_type=F32)
    first, second = score[:, :C_HALF], score[:, C_HALF:]
    keep_ref[...] = jnp.where(core == 0, first, second)
    send_ref[...] = jnp.where(core == 0, second, first)
    goal = jnp.concatenate([p[:, K_DEV:] for p in ps], 0).astype(F32)
    goal_ref[...] = jnp.broadcast_to(goal[:, :1] * 16.0 + goal[:, 64:65], (E_ALL, 128))


def sum_body(a0, a1, a2, a3, s0, s1, s2, s3):
    score = (a0[...] + a1[...]) + (a2[...] + a3[...])
    for d, ref in enumerate((s0, s1, s2, s3)):
        ref[...] = score[d * E_DEV : (d + 1) * E_DEV]


def total_body(s0, s1, s2, s3, goal_ref, slots_ref):
    core, y = lax.axis_index("core"), lax.axis_index("y")
    score = jnp.concatenate([s[...] for s in (s0, s1, s2, s3)], 0)
    first = ((y * NC + core) * C_HALF).astype(F32)
    goal = goal_ref[...] - first
    lane = lax.broadcasted_iota(I32, (E_ALL, 128), 1).astype(F32)
    pieces = []
    for j in range(C_HALF // 128):
        hit = goal == lane + 128.0 * j
        sums = jnp.sum(jnp.where(hit, score[:, 128 * j : 128 * (j + 1)], 0.0), 0, keepdims=True)
        pieces += [sums[:, i * C_DEV : (i + 1) * C_DEV] for i in range(128 // C_DEV) for _ in range(NC)]
    rows = jnp.concatenate(pieces, 0)
    for c in range(NC):
        slots_ref[c * len(pieces) : (c + 1) * len(pieces)] = jnp.where(core == c, rows, 0.0)


def lay_body(mine_ref, other_ref, flag_ref, own_flag_ref, slots_ref, out_ref, total_ref):
    core, y, z = (lax.axis_index(name) for name in ("core", "y", "z"))
    for d in range(NY):
        for part, ref in ((core, mine_ref), (1 - core, other_ref)):
            at = pl.ds(pl.multiple_of((y ^ d) * C_ALL + part * C_HALF, C_HALF), C_HALF)
            out_ref[:, at] = ref[d * E_DEV : (d + 1) * E_DEV, :] * flag_ref[:, at].astype(F32)
    flags = own_flag_ref[pl.ds(y * NZ + z, 1), :].astype(F32)
    total_ref[...] = jnp.sum(slots_ref[...], 0, keepdims=True) * flags


def per_device(
    down_matrix_feeds,
    result_slope_matrix,
    feed_sketch_factor,
    result_slope_factor,
    heldout_slope_entries,
    objective_of_sample,
    kept_choice_flags,
    token_sample_position,
):
    far = swap(heldout_slope_entries[None], "z", 7)
    keep, away, held = project(
        down_matrix_feeds,
        result_slope_matrix,
        feed_sketch_factor.T,
        result_slope_factor.T,
        heldout_slope_entries,
    )
    held = jnp.concatenate([held[None], far], 0)
    far = swap(held, "z", 2)

    sent = shaped(2 * ROWS + HALF, TOK, dtype=I16)
    low, half = shaped(ROWS, TOK), shaped(HALF, TOK)
    s1, s2, s3, in_own, out_chip = call(
        spread_body, [sent, sent, sent, low, half], keep, swap(away, "core", 1)
    )
    got = {d: swap(s, "x", d) for d, s in ((2, s2), (1, s1), (3, s3))}
    held = call(join_body, shaped(NZ // 2, C_DEV, K_DEV, dtype=BF16), held, far, after=in_own)
    far = swap(held, "z", 1)
    in_sum, out_half = call(add_body, [low, half], in_own, out_chip, got[1], got[2], got[3])
    packed = call(
        outer_body,
        shaped(E_DEV, K_DEV + 128, dtype=BF16),
        in_sum,
        out_half,
        swap(out_half, "core", 1),
        token_sample_position,
        objective_of_sample[:, None],
        work=400000000,
    )
    packs = {d: swap(packed, "y", d) for d in (2, 1, 3)}

    side = shaped(E_ALL, C_HALF)
    keep, send, goal = call(
        score_body,
        [side, side, shaped(E_ALL, 128)],
        packed,
        packs[1],
        packs[2],
        packs[3],
        held,
        far,
        scratch=[pltpu.VMEM((C_ALL, K_DEV), BF16)],
    )
    score = keep + swap(send, "core", 1)
    got = {d: swap(score, "x", d) for d in (2, 1, 3)}
    piece = shaped(E_DEV, C_HALF)
    pieces = call(sum_body, [piece] * NY, score, got[1], got[2], got[3])
    slots = call(total_body, shaped(NZ * NC, C_DEV), *pieces, goal)
    got = {d: swap(pieces[d], "y", d) for d in (2, 1, 3)}
    mine = jnp.concatenate([pieces[0], got[1], got[2], got[3]], 0)
    mine, slots = lax.optimization_barrier((mine, slots))
    sample_affinity, totals = call(
        lay_body,
        [shaped(E_DEV, CHOICES), shaped(1, C_DEV)],
        mine,
        swap(mine, "core", 1),
        kept_choice_flags.reshape(1, CHOICES),
        kept_choice_flags.reshape(NY * NZ, C_DEV),
        lax.all_to_all(slots, ("z", "core"), 0, 0, tiled=True),
    )
    return (sample_affinity, totals[0])


def solution(mesh):
    ex, tp = ("y", "z"), ("x", "core")
    chips = Mesh(mesh.devices.reshape(NY, NZ, NX, NC), ("y", "z", "x", "core"))
    placed = (
        P(ex, tp),
        P(ex, tp),
        P(tp, None),
        P(tp, None),
        P(ex, tp),
        P(ex),
        P(),
        P(ex, None),
    )
    return jax.shard_map(
        per_device, mesh=chips, in_specs=placed, out_specs=(P(ex, None), P(ex)), check_vma=False
    )
```

```python
import jax
import jax.numpy as jnp
from jax import lax
from jax.experimental import pallas as pl
from jax.experimental.pallas import tpu as pltpu
from jax.sharding import Mesh
from jax.sharding import PartitionSpec as P

NY, NZ, NX, NC = 4, 8, 4, 2
SIZES = dict(y=NY, z=NZ, x=NX, core=NC)
RANK, TOK, E_DEV, C_DEV, K_DEV, CHOICES = 64, 1024, 16, 64, 512, 2048
ROWS = RANK // (NX * NC)
HALF = RANK // 2
E_ALL, C_ALL = NY * E_DEV, NZ * C_DEV
C_HALF = C_ALL // NC
F32, BF16, I32, I16 = jnp.float32, jnp.bfloat16, jnp.int32, jnp.int16
NT = (((1,), (1,)), ((), ()))
CHUNK = 512
VMEM_LIMIT = 48 * 1024 * 1024


def swap(value, axis, bits):
    return lax.ppermute(value, axis, [(i, i ^ bits) for i in range(SIZES[axis])])


def shaped(*dims, dtype=F32):
    return jax.ShapeDtypeStruct(dims, dtype)


def call(body, outs, *args, scratch=(), after=None, work=0):
    count = len(args)
    specs = [pl.BlockSpec(memory_space=pltpu.VMEM)] * count
    run = body
    if after is not None:
        run = lambda *refs: body(*refs[:count], *refs[count + 1 :])
        specs, args = specs + [pl.BlockSpec(memory_space=pl.ANY)], args + (after,)
    return pl.pallas_call(
        run,
        out_shape=outs,
        in_specs=specs,
        scratch_shapes=scratch,
        compiler_params=pltpu.CompilerParams(vmem_limit_bytes=VMEM_LIMIT),
        cost_estimate=pl.CostEstimate(flops=work, transcendentals=0, bytes_accessed=work // 100) if work else None,
    )(*args)


def project_body(
    x_hbm, y_hbm, w_in_hbm, w_out_hbm, h_hbm, keep_ref, send_ref, h_ref, parts, w_in, w_out, low, out, sems
):
    core = lax.axis_index("core")
    steps = [(y_hbm, w_out, out, k) for k in range(y_hbm.shape[1] // CHUNK)]
    steps += [(x_hbm, w_in, low, k) for k in range(x_hbm.shape[1] // CHUNK)]
    copies = [
        pltpu.make_async_copy(src.at[:, pl.ds(k * CHUNK, CHUNK)], parts.at[n], sems.at[n])
        for n, (src, _, _, k) in enumerate(steps)
    ]
    copy_out = pltpu.make_async_copy(w_out_hbm, w_out, sems.at[len(steps)])
    copy_in = pltpu.make_async_copy(w_in_hbm, w_in, sems.at[len(steps) + 1])
    copy_out.start()
    copies[0].start()
    copy_in.start()
    for copy in copies[1:]:
        copy.start()
    copy_held = pltpu.make_async_copy(h_hbm, h_ref, sems.at[len(steps) + 2])
    copy_held.start()
    copy_out.wait()
    for n, (src, weights, total, k) in enumerate(steps):
        copies[n].wait()
        if src is x_hbm and k == 0:
            copy_in.wait()
        part = lax.dot_general(
            weights[:, k * CHUNK : (k + 1) * CHUNK], parts[n], NT, preferred_element_type=F32
        )
        if k == 0:
            total[...] = part
        else:
            total[...] += part
    copy_held.wait()
    for c in range(NC):
        part = [low[(NC * j + c) * ROWS : (NC * j + c + 1) * ROWS] for j in range(NX)]
        part = jnp.concatenate(part + [out[c * HALF : (c + 1) * HALF]], 0)

        @pl.when(core == c)
        def _():
            keep_ref[...] = part

        @pl.when(core != c)
        def _():
            send_ref[...] = part


def project(x, y, w_in, w_out, held):
    steps = (x.shape[1] + y.shape[1]) // CHUNK
    args = [pltpu.with_memory_space_constraint(a, pltpu.HBM) for a in (x, y, w_in, w_out, held)]
    return pl.pallas_call(
        project_body,
        in_specs=[pl.BlockSpec(memory_space=pltpu.HBM)] * 5,
        out_shape=[shaped(RANK, TOK), shaped(RANK, TOK), shaped(*held.shape, dtype=BF16)],
        scratch_shapes=[
            pltpu.VMEM((steps, TOK, CHUNK), BF16),
            pltpu.VMEM(w_in.shape, BF16),
            pltpu.VMEM(w_out.shape, BF16),
            pltpu.VMEM((RANK, TOK), F32),
            pltpu.VMEM((RANK, TOK), F32),
            pltpu.SemaphoreType.DMA((steps + 3,)),
        ],
        compiler_params=pltpu.CompilerParams(vmem_limit_bytes=VMEM_LIMIT),
        cost_estimate=pl.CostEstimate(
            flops=2 * RANK * x.size + 2 * RANK * y.size, transcendentals=0, bytes_accessed=2 * (x.size + y.size)
        ),
    )(*args)


def coded(value):
    top = jnp.maximum(jnp.max(jnp.abs(value), 0, keepdims=True), 1e-30)
    power = jnp.clip(jnp.floor(jnp.log2(top)) - 13.0, -100.0, 100.0)
    return jnp.round(value / jnp.exp2(power)), power


def spread_body(keep_ref, got_ref, s1_ref, s2_ref, s3_ref, in_ref, out_ref):
    x = lax.axis_index("x")
    out = keep_ref[NX * ROWS :] + got_ref[NX * ROWS :]
    out_ref[...] = out
    out_code, out_power = coded(out)
    line = lax.broadcasted_iota(I32, (ROWS, TOK), 0)
    for d, ref in ((1, s1_ref), (2, s2_ref), (3, s3_ref), (0, None)):
        at = pl.ds(pl.multiple_of((x ^ d) * ROWS, ROWS), ROWS)
        part = keep_ref[at, :] + got_ref[at, :]
        if ref is None:
            in_ref[...] = part
        else:
            code, power = coded(part)
            powers = jnp.where(line == 0, power, out_power)
            ref[...] = jnp.concatenate([code, out_code, powers], 0).astype(I32).astype(I16)


def join_body(first_ref, second_ref, out_ref):
    out_ref[: first_ref.shape[0]] = first_ref[...]
    out_ref[first_ref.shape[0] :] = second_ref[...]


def add_body(in_ref, out_ref, g2_ref, g1_ref, g3_ref, low_ref, half_ref):
    low, half = in_ref[...], out_ref[...]
    for ref in (g1_ref, g2_ref, g3_ref):
        got = ref[...].astype(I32).astype(F32)
        powers = jnp.exp2(got[ROWS + HALF :])
        low = low + got[:ROWS] * powers[:1]
        half = half + got[ROWS : ROWS + HALF] * powers[1:2]
    low_ref[...] = low
    half_ref[...] = half


def parts_of(value):
    high = value.astype(BF16)
    return high, (value - high.astype(F32)).astype(BF16)


def outer_body(in_ref, mine_ref, other_ref, where_ref, goal_ref, p_ref):
    core = lax.axis_index("core")
    low, mine, other = in_ref[...], mine_ref[...], other_ref[...]
    out = jnp.concatenate([jnp.where(core == 0, mine, other), jnp.where(core == 0, other, mine)], 0)
    out_high, out_low = parts_of(out)
    onehot = lax.broadcasted_iota(I32, (E_DEV, TOK), 0) == where_ref[...]
    pairs = [parts_of(jnp.where(onehot, low[i : i + 1], 0.0)) for i in range(ROWS)]
    high = jnp.concatenate([p[0] for p in pairs], 0)
    rest = jnp.concatenate([p[1] for p in pairs], 0)
    dot = lambda u, v: lax.dot_general(u, v, NT, preferred_element_type=F32)
    grads = dot(high, out_high) + (dot(high, out_low) + dot(rest, out_high))
    flat = [grads[i * E_DEV : (i + 1) * E_DEV] for i in range(ROWS)]
    goal = jnp.broadcast_to(goal_ref[...], (E_DEV, 128))
    goal = jnp.where(lax.broadcasted_iota(I32, (E_DEV, 128), 1) < 64, goal >> 4, goal & 15)
    p_ref[...] = jnp.concatenate(flat + [goal.astype(F32)], 1).astype(BF16)


def score_body(p0, p2, p1, p3, first_ref, second_ref, keep_ref, send_ref, goal_ref, held):
    core, z = lax.axis_index("core"), lax.axis_index("z")
    for m, bits in enumerate((0, 7, 2, 5, 1, 6, 3, 4)):
        at = pl.ds(pl.multiple_of((z ^ bits) * C_DEV, C_DEV), C_DEV)
        held[at, :] = (first_ref, second_ref)[m // (NZ // 2)][m % (NZ // 2)]
    ps = [p[...] for p in (p0, p1, p2, p3)]
    left = jnp.concatenate([p[:, :K_DEV] for p in ps], 0)
    score = lax.dot_general(left, held[...], NT, preferred_element_type=F32)
    first, second = score[:, :C_HALF], score[:, C_HALF:]
    keep_ref[...] = jnp.where(core == 0, first, second)
    send_ref[...] = jnp.where(core == 0, second, first)
    goal = jnp.concatenate([p[:, K_DEV:] for p in ps], 0).astype(F32)
    goal_ref[...] = jnp.broadcast_to(goal[:, :1] * 16.0 + goal[:, 64:65], (E_ALL, 128))


def sum_body(a0, a2, a1, a3, s0, s1, s2, s3):
    score = (a0[...] + a1[...]) + (a2[...] + a3[...])
    for d, ref in enumerate((s0, s1, s2, s3)):
        ref[...] = score[d * E_DEV : (d + 1) * E_DEV]


def total_body(s0, s1, s2, s3, goal_ref, slots_ref):
    core, y = lax.axis_index("core"), lax.axis_index("y")
    score = jnp.concatenate([s[...] for s in (s0, s1, s2, s3)], 0)
    first = ((y * NC + core) * C_HALF).astype(F32)
    goal = goal_ref[...] - first
    lane = lax.broadcasted_iota(I32, (E_ALL, 128), 1).astype(F32)
    pieces = []
    for j in range(C_HALF // 128):
        hit = goal == lane + 128.0 * j
        sums = jnp.sum(jnp.where(hit, score[:, 128 * j : 128 * (j + 1)], 0.0), 0, keepdims=True)
        pieces += [sums[:, i * C_DEV : (i + 1) * C_DEV] for i in range(128 // C_DEV) for _ in range(NC)]
    rows = jnp.concatenate(pieces, 0)
    for c in range(NC):
        slots_ref[c * len(pieces) : (c + 1) * len(pieces)] = jnp.where(core == c, rows, 0.0)


def lay_body(mine_ref, other_ref, flag_ref, own_flag_ref, slots_ref, out_ref, total_ref):
    core, y, z = (lax.axis_index(name) for name in ("core", "y", "z"))
    for n, d in enumerate((0, 2, 1, 3)):
        for part, ref in ((core, mine_ref), (1 - core, other_ref)):
            at = pl.ds(pl.multiple_of((y ^ d) * C_ALL + part * C_HALF, C_HALF), C_HALF)
            out_ref[:, at] = ref[n * E_DEV : (n + 1) * E_DEV, :] * flag_ref[:, at].astype(F32)
    flags = own_flag_ref[pl.ds(y * NZ + z, 1), :].astype(F32)
    total_ref[...] = jnp.sum(slots_ref[...], 0, keepdims=True) * flags


def per_device(
    down_matrix_feeds,
    result_slope_matrix,
    feed_sketch_factor,
    result_slope_factor,
    heldout_slope_entries,
    objective_of_sample,
    kept_choice_flags,
    token_sample_position,
):
    far = swap(heldout_slope_entries[None], "z", 7)
    keep, away, held = project(
        down_matrix_feeds,
        result_slope_matrix,
        feed_sketch_factor.T,
        result_slope_factor.T,
        heldout_slope_entries,
    )
    held = jnp.concatenate([held[None], far], 0)
    far = swap(held, "z", 2)

    sent = shaped(2 * ROWS + HALF, TOK, dtype=I16)
    low, half = shaped(ROWS, TOK), shaped(HALF, TOK)
    s1, s2, s3, in_own, out_chip = call(
        spread_body, [sent, sent, sent, low, half], keep, swap(away, "core", 1)
    )
    got = {d: swap(s, "x", d) for d, s in ((2, s2), (1, s1), (3, s3))}
    held = call(join_body, shaped(NZ // 2, C_DEV, K_DEV, dtype=BF16), held, far, after=in_own)
    far = swap(held, "z", 1)
    in_sum, out_half = call(add_body, [low, half], in_own, out_chip, got[2], got[1], got[3])
    packed = call(
        outer_body,
        shaped(E_DEV, K_DEV + 128, dtype=BF16),
        in_sum,
        out_half,
        swap(out_half, "core", 1),
        token_sample_position,
        objective_of_sample[:, None],
        work=400000000,
    )
    packs = {d: swap(packed, "y", d) for d in (2, 1, 3)}

    side = shaped(E_ALL, C_HALF)
    keep, send, goal = call(
        score_body,
        [side, side, shaped(E_ALL, 128)],
        packed,
        packs[2],
        packs[1],
        packs[3],
        held,
        far,
        scratch=[pltpu.VMEM((C_ALL, K_DEV), BF16)],
    )
    score = keep + swap(send, "core", 1)
    got = {d: swap(score, "x", d) for d in (2, 1, 3)}
    piece = shaped(E_DEV, C_HALF)
    pieces = call(sum_body, [piece] * NY, score, got[2], got[1], got[3])
    slots = call(total_body, shaped(NZ * NC, C_DEV), *pieces, goal)
    got = {d: swap(pieces[d], "y", d) for d in (2, 1, 3)}
    mine = jnp.concatenate([pieces[0], got[2], got[1], got[3]], 0)
    mine, slots = lax.optimization_barrier((mine, slots))
    sample_affinity, totals = call(
        lay_body,
        [shaped(E_DEV, CHOICES), shaped(1, C_DEV)],
        mine,
        swap(mine, "core", 1),
        kept_choice_flags.reshape(1, CHOICES),
        kept_choice_flags.reshape(NY * NZ, C_DEV),
        lax.all_to_all(slots, ("z", "core"), 0, 0, tiled=True),
    )
    return (sample_affinity, totals[0])


def solution(mesh):
    ex, tp = ("y", "z"), ("x", "core")
    chips = Mesh(mesh.devices.reshape(NY, NZ, NX, NC), ("y", "z", "x", "core"))
    placed = (
        P(ex, tp),
        P(ex, tp),
        P(tp, None),
        P(tp, None),
        P(ex, tp),
        P(ex),
        P(),
        P(ex, None),
    )
    return jax.shard_map(
        per_device, mesh=chips, in_specs=placed, out_specs=(P(ex, None), P(ex)), check_vma=False
    )
```

```python
import jax
import jax.numpy as jnp
from jax import lax
from jax.experimental import pallas as pl
from jax.experimental.pallas import tpu as pltpu
from jax.sharding import Mesh
from jax.sharding import PartitionSpec as P

NY, NZ, NX, NC = 4, 8, 4, 2
SIZES = dict(y=NY, z=NZ, x=NX, core=NC)
RANK, TOK, E_DEV, C_DEV, K_DEV, CHOICES = 64, 1024, 16, 64, 512, 2048
ROWS = RANK // (NX * NC)
HALF = RANK // 2
E_ALL, C_ALL = NY * E_DEV, NZ * C_DEV
C_HALF = C_ALL // NC
F32, BF16, I32, I16 = jnp.float32, jnp.bfloat16, jnp.int32, jnp.int16
NT = (((1,), (1,)), ((), ()))
CHUNK = 512
VMEM_LIMIT = 48 * 1024 * 1024


def swap(value, axis, bits):
    return lax.ppermute(value, axis, [(i, i ^ bits) for i in range(SIZES[axis])])


def shaped(*dims, dtype=F32):
    return jax.ShapeDtypeStruct(dims, dtype)


def call(body, outs, *args, scratch=(), after=None, work=0):
    count = len(args)
    specs = [pl.BlockSpec(memory_space=pltpu.VMEM)] * count
    run = body
    if after is not None:
        run = lambda *refs: body(*refs[:count], *refs[count + 1 :])
        specs, args = specs + [pl.BlockSpec(memory_space=pl.ANY)], args + (after,)
    return pl.pallas_call(
        run,
        out_shape=outs,
        in_specs=specs,
        scratch_shapes=scratch,
        compiler_params=pltpu.CompilerParams(vmem_limit_bytes=VMEM_LIMIT),
        cost_estimate=pl.CostEstimate(flops=work, transcendentals=0, bytes_accessed=work // 100) if work else None,
    )(*args)


def project_body(
    x_hbm, y_hbm, w_in_hbm, w_out_hbm, h_hbm, keep_ref, send_ref, h_ref, parts, w_in, w_out, low, out, sems
):
    core = lax.axis_index("core")
    steps = [(y_hbm, w_out, out, k) for k in range(y_hbm.shape[1] // CHUNK)]
    steps += [(x_hbm, w_in, low, k) for k in range(x_hbm.shape[1] // CHUNK)]
    copies = [
        pltpu.make_async_copy(src.at[:, pl.ds(k * CHUNK, CHUNK)], parts.at[n], sems.at[n])
        for n, (src, _, _, k) in enumerate(steps)
    ]
    copy_out = pltpu.make_async_copy(w_out_hbm, w_out, sems.at[len(steps)])
    copy_in = pltpu.make_async_copy(w_in_hbm, w_in, sems.at[len(steps) + 1])
    copy_out.start()
    copies[0].start()
    copy_in.start()
    for copy in copies[1:]:
        copy.start()
    copy_held = pltpu.make_async_copy(h_hbm, h_ref, sems.at[len(steps) + 2])
    copy_held.start()
    copy_out.wait()
    for n, (src, weights, total, k) in enumerate(steps):
        copies[n].wait()
        if src is x_hbm and k == 0:
            copy_in.wait()
        part = lax.dot_general(
            weights[:, k * CHUNK : (k + 1) * CHUNK], parts[n], NT, preferred_element_type=F32
        )
        if k == 0:
            total[...] = part
        else:
            total[...] += part
    copy_held.wait()
    for c in range(NC):
        part = [low[(NC * j + c) * ROWS : (NC * j + c + 1) * ROWS] for j in range(NX)]
        part = jnp.concatenate(part + [out[c * HALF : (c + 1) * HALF]], 0)

        @pl.when(core == c)
        def _():
            keep_ref[...] = part

        @pl.when(core != c)
        def _():
            send_ref[...] = part


def project(x, y, w_in, w_out, held):
    steps = (x.shape[1] + y.shape[1]) // CHUNK
    args = [pltpu.with_memory_space_constraint(a, pltpu.HBM) for a in (x, y, w_in, w_out, held)]
    return pl.pallas_call(
        project_body,
        in_specs=[pl.BlockSpec(memory_space=pltpu.HBM)] * 5,
        out_shape=[shaped(RANK, TOK), shaped(RANK, TOK), shaped(*held.shape, dtype=BF16)],
        scratch_shapes=[
            pltpu.VMEM((steps, TOK, CHUNK), BF16),
            pltpu.VMEM(w_in.shape, BF16),
            pltpu.VMEM(w_out.shape, BF16),
            pltpu.VMEM((RANK, TOK), F32),
            pltpu.VMEM((RANK, TOK), F32),
            pltpu.SemaphoreType.DMA((steps + 3,)),
        ],
        compiler_params=pltpu.CompilerParams(vmem_limit_bytes=VMEM_LIMIT),
        cost_estimate=pl.CostEstimate(
            flops=2 * RANK * x.size + 2 * RANK * y.size, transcendentals=0, bytes_accessed=2 * (x.size + y.size)
        ),
    )(*args)


def coded(value):
    top = jnp.maximum(jnp.max(jnp.abs(value), 0, keepdims=True), 1e-30)
    power = jnp.clip(jnp.floor(jnp.log2(top)) - 13.0, -100.0, 100.0)
    return jnp.round(value / jnp.exp2(power)), power


def spread_body(keep_ref, got_ref, s1_ref, s2_ref, s3_ref, in_ref, out_ref):
    x = lax.axis_index("x")
    out = keep_ref[NX * ROWS :] + got_ref[NX * ROWS :]
    out_ref[...] = out
    out_code, out_power = coded(out)
    line = lax.broadcasted_iota(I32, (ROWS, TOK), 0)
    for d, ref in ((1, s1_ref), (2, s2_ref), (3, s3_ref), (0, None)):
        at = pl.ds(pl.multiple_of((x ^ d) * ROWS, ROWS), ROWS)
        part = keep_ref[at, :] + got_ref[at, :]
        if ref is None:
            in_ref[...] = part
        else:
            code, power = coded(part)
            powers = jnp.where(line == 0, power, out_power)
            ref[...] = jnp.concatenate([code, out_code, powers], 0).astype(I32).astype(I16)


def join_body(first_ref, second_ref, out_ref):
    out_ref[: first_ref.shape[0]] = first_ref[...]
    out_ref[first_ref.shape[0] :] = second_ref[...]


def add_body(in_ref, out_ref, g2_ref, g1_ref, g3_ref, low_ref, half_ref):
    low, half = in_ref[...], out_ref[...]
    for ref in (g1_ref, g2_ref, g3_ref):
        got = ref[...].astype(I32).astype(F32)
        powers = jnp.exp2(got[ROWS + HALF :])
        low = low + got[:ROWS] * powers[:1]
        half = half + got[ROWS : ROWS + HALF] * powers[1:2]
    low_ref[...] = low
    half_ref[...] = half


def parts_of(value):
    high = value.astype(BF16)
    return high, (value - high.astype(F32)).astype(BF16)


def outer_body(in_ref, mine_ref, other_ref, where_ref, goal_ref, p_ref):
    core = lax.axis_index("core")
    low, mine, other = in_ref[...], mine_ref[...], other_ref[...]
    out = jnp.concatenate([jnp.where(core == 0, mine, other), jnp.where(core == 0, other, mine)], 0)
    out_high, out_low = parts_of(out)
    onehot = lax.broadcasted_iota(I32, (E_DEV, TOK), 0) == where_ref[...]
    pairs = [parts_of(jnp.where(onehot, low[i : i + 1], 0.0)) for i in range(ROWS)]
    high = jnp.concatenate([p[0] for p in pairs], 0)
    rest = jnp.concatenate([p[1] for p in pairs], 0)
    dot = lambda u, v: lax.dot_general(u, v, NT, preferred_element_type=F32)
    grads = dot(high, out_high) + (dot(high, out_low) + dot(rest, out_high))
    flat = [grads[i * E_DEV : (i + 1) * E_DEV] for i in range(ROWS)]
    goal = jnp.broadcast_to(goal_ref[...], (E_DEV, 128))
    goal = jnp.where(lax.broadcasted_iota(I32, (E_DEV, 128), 1) < 64, goal >> 4, goal & 15)
    p_ref[...] = jnp.concatenate(flat + [goal.astype(F32)], 1).astype(BF16)


def score_body(p0, p2, p1, p3, first_ref, second_ref, keep_ref, send_ref, goal_ref, held):
    core, z = lax.axis_index("core"), lax.axis_index("z")
    for m, bits in enumerate((0, 7, 2, 5, 1, 6, 3, 4)):
        at = pl.ds(pl.multiple_of((z ^ bits) * C_DEV, C_DEV), C_DEV)
        held[at, :] = (first_ref, second_ref)[m // (NZ // 2)][m % (NZ // 2)]
    ps = [p[...] for p in (p0, p1, p2, p3)]
    left = jnp.concatenate([p[:, :K_DEV] for p in ps], 0)
    score = lax.dot_general(left, held[...], NT, preferred_element_type=F32)
    first, second = score[:, :C_HALF], score[:, C_HALF:]
    keep_ref[...] = jnp.where(core == 0, first, second)
    send_ref[...] = jnp.where(core == 0, second, first)
    goal = jnp.concatenate([p[:, K_DEV:] for p in ps], 0).astype(F32)
    goal_ref[...] = jnp.broadcast_to(goal[:, :1] * 16.0 + goal[:, 64:65], (E_ALL, 128))


def pack_body(keep_ref, got_ref, code_ref):
    code, power = coded(keep_ref[...] + got_ref[...])
    power = jnp.broadcast_to(power, (2 * ROWS, C_HALF))
    code_ref[...] = jnp.concatenate([code, power], 0).astype(I32).astype(I16)


def sum_body(a0, a2, a1, a3, s0, s1, s2, s3):
    parts = []
    for ref in (a0, a1, a2, a3):
        got = ref[...].astype(I32).astype(F32)
        parts.append(got[:E_ALL] * jnp.exp2(got[E_ALL : E_ALL + 1]))
    score = (parts[0] + parts[1]) + (parts[2] + parts[3])
    for d, ref in enumerate((s0, s1, s2, s3)):
        ref[...] = score[d * E_DEV : (d + 1) * E_DEV]


def total_body(s0, s1, s2, s3, goal_ref, slots_ref):
    core, y = lax.axis_index("core"), lax.axis_index("y")
    score = jnp.concatenate([s[...] for s in (s0, s1, s2, s3)], 0)
    first = ((y * NC + core) * C_HALF).astype(F32)
    goal = goal_ref[...] - first
    lane = lax.broadcasted_iota(I32, (E_ALL, 128), 1).astype(F32)
    pieces = []
    for j in range(C_HALF // 128):
        hit = goal == lane + 128.0 * j
        sums = jnp.sum(jnp.where(hit, score[:, 128 * j : 128 * (j + 1)], 0.0), 0, keepdims=True)
        pieces += [sums[:, i * C_DEV : (i + 1) * C_DEV] for i in range(128 // C_DEV) for _ in range(NC)]
    rows = jnp.concatenate(pieces, 0)
    for c in range(NC):
        slots_ref[c * len(pieces) : (c + 1) * len(pieces)] = jnp.where(core == c, rows, 0.0)


def lay_body(mine_ref, other_ref, flag_ref, own_flag_ref, slots_ref, out_ref, total_ref):
    core, y, z = (lax.axis_index(name) for name in ("core", "y", "z"))
    for n, d in enumerate((0, 2, 1, 3)):
        for part, ref in ((core, mine_ref), (1 - core, other_ref)):
            at = pl.ds(pl.multiple_of((y ^ d) * C_ALL + part * C_HALF, C_HALF), C_HALF)
            out_ref[:, at] = ref[n * E_DEV : (n + 1) * E_DEV, :] * flag_ref[:, at].astype(F32)
    flags = own_flag_ref[pl.ds(y * NZ + z, 1), :].astype(F32)
    total_ref[...] = jnp.sum(slots_ref[...], 0, keepdims=True) * flags


def per_device(
    down_matrix_feeds,
    result_slope_matrix,
    feed_sketch_factor,
    result_slope_factor,
    heldout_slope_entries,
    objective_of_sample,
    kept_choice_flags,
    token_sample_position,
):
    far = swap(heldout_slope_entries[None], "z", 7)
    keep, away, held = project(
        down_matrix_feeds,
        result_slope_matrix,
        feed_sketch_factor.T,
        result_slope_factor.T,
        heldout_slope_entries,
    )
    held = jnp.concatenate([held[None], far], 0)
    far = swap(held, "z", 2)

    sent = shaped(2 * ROWS + HALF, TOK, dtype=I16)
    low, half = shaped(ROWS, TOK), shaped(HALF, TOK)
    s1, s2, s3, in_own, out_chip = call(
        spread_body, [sent, sent, sent, low, half], keep, swap(away, "core", 1)
    )
    got = {d: swap(s, "x", d) for d, s in ((2, s2), (1, s1), (3, s3))}
    held = call(join_body, shaped(NZ // 2, C_DEV, K_DEV, dtype=BF16), held, far, after=in_own)
    far = swap(held, "z", 1)
    in_sum, out_half = call(add_body, [low, half], in_own, out_chip, got[2], got[1], got[3])
    packed = call(
        outer_body,
        shaped(E_DEV, K_DEV + 128, dtype=BF16),
        in_sum,
        out_half,
        swap(out_half, "core", 1),
        token_sample_position,
        objective_of_sample[:, None],
        work=400000000,
    )
    packs = {d: swap(packed, "y", d) for d in (2, 1, 3)}

    side = shaped(E_ALL, C_HALF)
    keep, send, goal = call(
        score_body,
        [side, side, shaped(E_ALL, 128)],
        packed,
        packs[2],
        packs[1],
        packs[3],
        held,
        far,
        scratch=[pltpu.VMEM((C_ALL, K_DEV), BF16)],
    )
    score = call(
        pack_body, shaped(E_ALL + 2 * ROWS, C_HALF, dtype=I16), keep, swap(send, "core", 1)
    )
    got = {d: swap(score, "x", d) for d in (2, 1, 3)}
    piece = shaped(E_DEV, C_HALF)
    pieces = call(sum_body, [piece] * NY, score, got[2], got[1], got[3])
    slots = call(total_body, shaped(NZ * NC, C_DEV), *pieces, goal)
    got = {d: swap(pieces[d], "y", d) for d in (2, 1, 3)}
    mine = jnp.concatenate([pieces[0], got[2], got[1], got[3]], 0)
    mine, slots = lax.optimization_barrier((mine, slots))
    sample_affinity, totals = call(
        lay_body,
        [shaped(E_DEV, CHOICES), shaped(1, C_DEV)],
        mine,
        swap(mine, "core", 1),
        kept_choice_flags.reshape(1, CHOICES),
        kept_choice_flags.reshape(NY * NZ, C_DEV),
        lax.all_to_all(slots, ("z", "core"), 0, 0, tiled=True),
    )
    return (sample_affinity, totals[0])


def solution(mesh):
    ex, tp = ("y", "z"), ("x", "core")
    chips = Mesh(mesh.devices.reshape(NY, NZ, NX, NC), ("y", "z", "x", "core"))
    placed = (
        P(ex, tp),
        P(ex, tp),
        P(tp, None),
        P(tp, None),
        P(ex, tp),
        P(ex),
        P(),
        P(ex, None),
    )
    return jax.shard_map(
        per_device, mesh=chips, in_specs=placed, out_specs=(P(ex, None), P(ex)), check_vma=False
    )
```

```python
import jax
import jax.numpy as jnp
from jax import lax
from jax.experimental import pallas as pl
from jax.experimental.pallas import tpu as pltpu
from jax.sharding import Mesh
from jax.sharding import PartitionSpec as P

NY, NZ, NX, NC = 4, 8, 4, 2
SIZES = dict(y=NY, z=NZ, x=NX, core=NC)
RANK, TOK, E_DEV, C_DEV, K_DEV, CHOICES = 64, 1024, 16, 64, 512, 2048
ROWS = RANK // (NX * NC)
HALF = RANK // 2
E_ALL, C_ALL = NY * E_DEV, NZ * C_DEV
C_HALF = C_ALL // NC
F32, BF16, I32, I16 = jnp.float32, jnp.bfloat16, jnp.int32, jnp.int16
NT = (((1,), (1,)), ((), ()))
CHUNK = 512
VMEM_LIMIT = 48 * 1024 * 1024


def swap(value, axis, bits):
    return lax.ppermute(value, axis, [(i, i ^ bits) for i in range(SIZES[axis])])


def shaped(*dims, dtype=F32):
    return jax.ShapeDtypeStruct(dims, dtype)


def call(body, outs, *args, scratch=(), after=None, work=0):
    count = len(args)
    specs = [pl.BlockSpec(memory_space=pltpu.VMEM)] * count
    run = body
    if after is not None:
        run = lambda *refs: body(*refs[:count], *refs[count + 1 :])
        specs, args = specs + [pl.BlockSpec(memory_space=pl.ANY)], args + (after,)
    return pl.pallas_call(
        run,
        out_shape=outs,
        in_specs=specs,
        scratch_shapes=scratch,
        compiler_params=pltpu.CompilerParams(vmem_limit_bytes=VMEM_LIMIT),
        cost_estimate=pl.CostEstimate(flops=work, transcendentals=0, bytes_accessed=work // 100) if work else None,
    )(*args)


def project_body(
    x_hbm, y_hbm, w_in_hbm, w_out_hbm, h_hbm, keep_ref, send_ref, h_ref, parts, w_in, w_out, low, out, sems
):
    core = lax.axis_index("core")
    steps = [(y_hbm, w_out, out, k) for k in range(y_hbm.shape[1] // CHUNK)]
    steps += [(x_hbm, w_in, low, k) for k in range(x_hbm.shape[1] // CHUNK)]
    copies = [
        pltpu.make_async_copy(src.at[:, pl.ds(k * CHUNK, CHUNK)], parts.at[n], sems.at[n])
        for n, (src, _, _, k) in enumerate(steps)
    ]
    copy_out = pltpu.make_async_copy(w_out_hbm, w_out, sems.at[len(steps)])
    copy_in = pltpu.make_async_copy(w_in_hbm, w_in, sems.at[len(steps) + 1])
    copy_out.start()
    copies[0].start()
    copy_in.start()
    for copy in copies[1:]:
        copy.start()
    copy_held = pltpu.make_async_copy(h_hbm, h_ref, sems.at[len(steps) + 2])
    copy_held.start()
    copy_out.wait()
    for n, (src, weights, total, k) in enumerate(steps):
        copies[n].wait()
        if src is x_hbm and k == 0:
            copy_in.wait()
        part = lax.dot_general(
            weights[:, k * CHUNK : (k + 1) * CHUNK], parts[n], NT, preferred_element_type=F32
        )
        if k == 0:
            total[...] = part
        else:
            total[...] += part
    copy_held.wait()
    for c in range(NC):
        part = [low[(NC * j + c) * ROWS : (NC * j + c + 1) * ROWS] for j in range(NX)]
        part = jnp.concatenate(part + [out[c * HALF : (c + 1) * HALF]], 0)

        @pl.when(core == c)
        def _():
            keep_ref[...] = part

        @pl.when(core != c)
        def _():
            send_ref[...] = part


def project(x, y, w_in, w_out, held):
    steps = (x.shape[1] + y.shape[1]) // CHUNK
    args = [pltpu.with_memory_space_constraint(a, pltpu.HBM) for a in (x, y, w_in, w_out, held)]
    return pl.pallas_call(
        project_body,
        in_specs=[pl.BlockSpec(memory_space=pltpu.HBM)] * 5,
        out_shape=[shaped(RANK, TOK), shaped(RANK, TOK), shaped(*held.shape, dtype=BF16)],
        scratch_shapes=[
            pltpu.VMEM((steps, TOK, CHUNK), BF16),
            pltpu.VMEM(w_in.shape, BF16),
            pltpu.VMEM(w_out.shape, BF16),
            pltpu.VMEM((RANK, TOK), F32),
            pltpu.VMEM((RANK, TOK), F32),
            pltpu.SemaphoreType.DMA((steps + 3,)),
        ],
        compiler_params=pltpu.CompilerParams(vmem_limit_bytes=VMEM_LIMIT),
        cost_estimate=pl.CostEstimate(
            flops=2 * RANK * x.size + 2 * RANK * y.size, transcendentals=0, bytes_accessed=2 * (x.size + y.size)
        ),
    )(*args)


def factors(power):
    half = jnp.floor(power * 0.5)
    return jnp.exp2(half), jnp.exp2(power - half)


def coded(value):
    top = jnp.maximum(jnp.max(jnp.abs(value), 0, keepdims=True), 1e-37)
    power = jnp.floor(jnp.log2(top)) - 13.0
    first, second = factors(power)
    return jnp.round(value / first / second), power


def decoded(code, power):
    first, second = factors(power)
    return code * first * second


def spread_body(keep_ref, got_ref, s1_ref, s2_ref, s3_ref, in_ref, out_ref):
    x = lax.axis_index("x")
    out = keep_ref[NX * ROWS :] + got_ref[NX * ROWS :]
    out_ref[...] = out
    out_code, out_power = coded(out)
    line = lax.broadcasted_iota(I32, (ROWS, TOK), 0)
    for d, ref in ((1, s1_ref), (2, s2_ref), (3, s3_ref), (0, None)):
        at = pl.ds(pl.multiple_of((x ^ d) * ROWS, ROWS), ROWS)
        part = keep_ref[at, :] + got_ref[at, :]
        if ref is None:
            in_ref[...] = part
        else:
            code, power = coded(part)
            powers = jnp.where(line == 0, power, out_power)
            ref[...] = jnp.concatenate([code, out_code, powers], 0).astype(I32).astype(I16)


def join_body(first_ref, second_ref, out_ref):
    out_ref[: first_ref.shape[0]] = first_ref[...]
    out_ref[first_ref.shape[0] :] = second_ref[...]


def add_body(in_ref, out_ref, g2_ref, g1_ref, g3_ref, low_ref, half_ref):
    low, half = in_ref[...], out_ref[...]
    for ref in (g1_ref, g2_ref, g3_ref):
        got = ref[...].astype(I32).astype(F32)
        powers = got[ROWS + HALF :]
        low = low + decoded(got[:ROWS], powers[:1])
        half = half + decoded(got[ROWS : ROWS + HALF], powers[1:2])
    low_ref[...] = low
    half_ref[...] = half


def parts_of(value):
    high = value.astype(BF16)
    return high, (value - high.astype(F32)).astype(BF16)


def outer_body(in_ref, mine_ref, other_ref, where_ref, goal_ref, p_ref):
    core = lax.axis_index("core")
    low, mine, other = in_ref[...], mine_ref[...], other_ref[...]
    out = jnp.concatenate([jnp.where(core == 0, mine, other), jnp.where(core == 0, other, mine)], 0)
    out_high, out_low = parts_of(out)
    onehot = lax.broadcasted_iota(I32, (E_DEV, TOK), 0) == where_ref[...]
    pairs = [parts_of(jnp.where(onehot, low[i : i + 1], 0.0)) for i in range(ROWS)]
    high = jnp.concatenate([p[0] for p in pairs], 0)
    rest = jnp.concatenate([p[1] for p in pairs], 0)
    dot = lambda u, v: lax.dot_general(u, v, NT, preferred_element_type=F32)
    grads = dot(high, out_high) + (dot(high, out_low) + dot(rest, out_high))
    flat = [grads[i * E_DEV : (i + 1) * E_DEV] for i in range(ROWS)]
    goal = jnp.broadcast_to(goal_ref[...], (E_DEV, 128))
    goal = jnp.where(lax.broadcasted_iota(I32, (E_DEV, 128), 1) < 64, goal >> 4, goal & 15)
    p_ref[...] = jnp.concatenate(flat + [goal.astype(F32)], 1).astype(BF16)


def score_body(p0, p2, p1, p3, first_ref, second_ref, keep_ref, send_ref, goal_ref, held):
    core, z = lax.axis_index("core"), lax.axis_index("z")
    for m, bits in enumerate((0, 7, 2, 5, 1, 6, 3, 4)):
        at = pl.ds(pl.multiple_of((z ^ bits) * C_DEV, C_DEV), C_DEV)
        held[at, :] = (first_ref, second_ref)[m // (NZ // 2)][m % (NZ // 2)]
    ps = [p[...] for p in (p0, p1, p2, p3)]
    left = jnp.concatenate([p[:, :K_DEV] for p in ps], 0)
    score = lax.dot_general(left, held[...], NT, preferred_element_type=F32)
    first, second = score[:, :C_HALF], score[:, C_HALF:]
    keep_ref[...] = jnp.where(core == 0, first, second)
    send_ref[...] = jnp.where(core == 0, second, first)
    goal = jnp.concatenate([p[:, K_DEV:] for p in ps], 0).astype(F32)
    goal_ref[...] = jnp.broadcast_to(goal[:, :1] * 16.0 + goal[:, 64:65], (E_ALL, 128))


def pack_body(keep_ref, got_ref, code_ref):
    code, power = coded(keep_ref[...] + got_ref[...])
    power = jnp.broadcast_to(power, (2 * ROWS, C_HALF))
    code_ref[...] = jnp.concatenate([code, power], 0).astype(I32).astype(I16)


def sum_body(a0, a2, a1, a3, s0, s1, s2, s3):
    parts = []
    for ref in (a0, a1, a2, a3):
        got = ref[...].astype(I32).astype(F32)
        parts.append(decoded(got[:E_ALL], got[E_ALL : E_ALL + 1]))
    score = (parts[0] + parts[1]) + (parts[2] + parts[3])
    for d, ref in enumerate((s0, s1, s2, s3)):
        ref[...] = score[d * E_DEV : (d + 1) * E_DEV]


def total_body(s0, s1, s2, s3, goal_ref, slots_ref):
    core, y = lax.axis_index("core"), lax.axis_index("y")
    score = jnp.concatenate([s[...] for s in (s0, s1, s2, s3)], 0)
    first = ((y * NC + core) * C_HALF).astype(F32)
    goal = goal_ref[...] - first
    lane = lax.broadcasted_iota(I32, (E_ALL, 128), 1).astype(F32)
    pieces = []
    for j in range(C_HALF // 128):
        hit = goal == lane + 128.0 * j
        sums = jnp.sum(jnp.where(hit, score[:, 128 * j : 128 * (j + 1)], 0.0), 0, keepdims=True)
        pieces += [sums[:, i * C_DEV : (i + 1) * C_DEV] for i in range(128 // C_DEV) for _ in range(NC)]
    rows = jnp.concatenate(pieces, 0)
    for c in range(NC):
        slots_ref[c * len(pieces) : (c + 1) * len(pieces)] = jnp.where(core == c, rows, 0.0)


def lay_body(mine_ref, other_ref, flag_ref, own_flag_ref, slots_ref, out_ref, total_ref):
    core, y, z = (lax.axis_index(name) for name in ("core", "y", "z"))
    for n, d in enumerate((0, 2, 1, 3)):
        for part, ref in ((core, mine_ref), (1 - core, other_ref)):
            at = pl.ds(pl.multiple_of((y ^ d) * C_ALL + part * C_HALF, C_HALF), C_HALF)
            out_ref[:, at] = ref[n * E_DEV : (n + 1) * E_DEV, :] * flag_ref[:, at].astype(F32)
    flags = own_flag_ref[pl.ds(y * NZ + z, 1), :].astype(F32)
    total_ref[...] = jnp.sum(slots_ref[...], 0, keepdims=True) * flags


def per_device(
    down_matrix_feeds,
    result_slope_matrix,
    feed_sketch_factor,
    result_slope_factor,
    heldout_slope_entries,
    objective_of_sample,
    kept_choice_flags,
    token_sample_position,
):
    far = swap(heldout_slope_entries[None], "z", 7)
    keep, away, held = project(
        down_matrix_feeds,
        result_slope_matrix,
        feed_sketch_factor.T,
        result_slope_factor.T,
        heldout_slope_entries,
    )
    held = jnp.concatenate([held[None], far], 0)
    far = swap(held, "z", 2)

    sent = shaped(2 * ROWS + HALF, TOK, dtype=I16)
    low, half = shaped(ROWS, TOK), shaped(HALF, TOK)
    s1, s2, s3, in_own, out_chip = call(
        spread_body, [sent, sent, sent, low, half], keep, swap(away, "core", 1)
    )
    got = {d: swap(s, "x", d) for d, s in ((2, s2), (1, s1), (3, s3))}
    held = call(join_body, shaped(NZ // 2, C_DEV, K_DEV, dtype=BF16), held, far, after=in_own)
    far = swap(held, "z", 1)
    in_sum, out_half = call(add_body, [low, half], in_own, out_chip, got[2], got[1], got[3])
    packed = call(
        outer_body,
        shaped(E_DEV, K_DEV + 128, dtype=BF16),
        in_sum,
        out_half,
        swap(out_half, "core", 1),
        token_sample_position,
        objective_of_sample[:, None],
        work=400000000,
    )
    packs = {d: swap(packed, "y", d) for d in (2, 1, 3)}

    side = shaped(E_ALL, C_HALF)
    keep, send, goal = call(
        score_body,
        [side, side, shaped(E_ALL, 128)],
        packed,
        packs[2],
        packs[1],
        packs[3],
        held,
        far,
        scratch=[pltpu.VMEM((C_ALL, K_DEV), BF16)],
    )
    score = call(
        pack_body, shaped(E_ALL + 2 * ROWS, C_HALF, dtype=I16), keep, swap(send, "core", 1)
    )
    got = {d: swap(score, "x", d) for d in (2, 1, 3)}
    piece = shaped(E_DEV, C_HALF)
    pieces = call(sum_body, [piece] * NY, score, got[2], got[1], got[3])
    slots = call(total_body, shaped(NZ * NC, C_DEV), *pieces, goal)
    got = {d: swap(pieces[d], "y", d) for d in (2, 1, 3)}
    mine = jnp.concatenate([pieces[0], got[2], got[1], got[3]], 0)
    mine, slots = lax.optimization_barrier((mine, slots))
    sample_affinity, totals = call(
        lay_body,
        [shaped(E_DEV, CHOICES), shaped(1, C_DEV)],
        mine,
        swap(mine, "core", 1),
        kept_choice_flags.reshape(1, CHOICES),
        kept_choice_flags.reshape(NY * NZ, C_DEV),
        lax.all_to_all(slots, ("z", "core"), 0, 0, tiled=True),
    )
    return (sample_affinity, totals[0])


def solution(mesh):
    ex, tp = ("y", "z"), ("x", "core")
    chips = Mesh(mesh.devices.reshape(NY, NZ, NX, NC), ("y", "z", "x", "core"))
    placed = (
        P(ex, tp),
        P(ex, tp),
        P(tp, None),
        P(tp, None),
        P(ex, tp),
        P(ex),
        P(),
        P(ex, None),
    )
    return jax.shard_map(
        per_device, mesh=chips, in_specs=placed, out_specs=(P(ex, None), P(ex)), check_vma=False
    )
```

```python
import jax
import jax.numpy as jnp
from jax import lax
from jax.experimental import pallas as pl
from jax.experimental.pallas import tpu as pltpu
from jax.sharding import Mesh
from jax.sharding import PartitionSpec as P

NY, NZ, NX, NC = 4, 8, 4, 2
SIZES = dict(y=NY, z=NZ, x=NX, core=NC)
RANK, TOK, E_DEV, C_DEV, K_DEV, CHOICES = 64, 1024, 16, 64, 512, 2048
ROWS = RANK // (NX * NC)
HALF = RANK // 2
E_ALL, C_ALL = NY * E_DEV, NZ * C_DEV
C_HALF = C_ALL // NC
F32, BF16, I32, I16 = jnp.float32, jnp.bfloat16, jnp.int32, jnp.int16
NT = (((1,), (1,)), ((), ()))
CHUNK = 512
VMEM_LIMIT = 48 * 1024 * 1024


def swap(value, axis, bits):
    return lax.ppermute(value, axis, [(i, i ^ bits) for i in range(SIZES[axis])])


def shaped(*dims, dtype=F32):
    return jax.ShapeDtypeStruct(dims, dtype)


def call(body, outs, *args, scratch=(), after=None, work=0):
    count = len(args)
    specs = [pl.BlockSpec(memory_space=pltpu.VMEM)] * count
    run = body
    if after is not None:
        run = lambda *refs: body(*refs[:count], *refs[count + 1 :])
        specs, args = specs + [pl.BlockSpec(memory_space=pl.ANY)], args + (after,)
    return pl.pallas_call(
        run,
        out_shape=outs,
        in_specs=specs,
        scratch_shapes=scratch,
        compiler_params=pltpu.CompilerParams(vmem_limit_bytes=VMEM_LIMIT),
        cost_estimate=pl.CostEstimate(flops=work, transcendentals=0, bytes_accessed=work // 100) if work else None,
    )(*args)


def project_body(
    x_hbm, y_hbm, w_in_hbm, w_out_hbm, h_hbm, keep_ref, send_ref, h_ref, parts, w_in, w_out, low, out, sems
):
    core = lax.axis_index("core")
    steps = [(y_hbm, w_out, out, k) for k in range(y_hbm.shape[1] // CHUNK)]
    steps += [(x_hbm, w_in, low, k) for k in range(x_hbm.shape[1] // CHUNK)]
    copies = [
        pltpu.make_async_copy(src.at[:, pl.ds(k * CHUNK, CHUNK)], parts.at[n], sems.at[n])
        for n, (src, _, _, k) in enumerate(steps)
    ]
    copy_out = pltpu.make_async_copy(w_out_hbm, w_out, sems.at[len(steps)])
    copy_in = pltpu.make_async_copy(w_in_hbm, w_in, sems.at[len(steps) + 1])
    copy_out.start()
    copies[0].start()
    copy_in.start()
    for copy in copies[1:]:
        copy.start()
    copy_held = pltpu.make_async_copy(h_hbm, h_ref, sems.at[len(steps) + 2])
    copy_held.start()
    copy_out.wait()
    for n, (src, weights, total, k) in enumerate(steps):
        copies[n].wait()
        if src is x_hbm and k == 0:
            copy_in.wait()
        part = lax.dot_general(
            weights[:, k * CHUNK : (k + 1) * CHUNK], parts[n], NT, preferred_element_type=F32
        )
        if k == 0:
            total[...] = part
        else:
            total[...] += part
    copy_held.wait()
    for c in range(NC):
        part = [low[(NC * j + c) * ROWS : (NC * j + c + 1) * ROWS] for j in range(NX)]
        part = jnp.concatenate(part + [out[c * HALF : (c + 1) * HALF]], 0)

        @pl.when(core == c)
        def _():
            keep_ref[...] = part

        @pl.when(core != c)
        def _():
            send_ref[...] = part


def project(x, y, w_in, w_out, held):
    steps = (x.shape[1] + y.shape[1]) // CHUNK
    args = [pltpu.with_memory_space_constraint(a, pltpu.HBM) for a in (x, y, w_in, w_out, held)]
    return pl.pallas_call(
        project_body,
        in_specs=[pl.BlockSpec(memory_space=pltpu.HBM)] * 5,
        out_shape=[shaped(RANK, TOK), shaped(RANK, TOK), shaped(*held.shape, dtype=BF16)],
        scratch_shapes=[
            pltpu.VMEM((steps, TOK, CHUNK), BF16),
            pltpu.VMEM(w_in.shape, BF16),
            pltpu.VMEM(w_out.shape, BF16),
            pltpu.VMEM((RANK, TOK), F32),
            pltpu.VMEM((RANK, TOK), F32),
            pltpu.SemaphoreType.DMA((steps + 3,)),
        ],
        compiler_params=pltpu.CompilerParams(vmem_limit_bytes=VMEM_LIMIT),
        cost_estimate=pl.CostEstimate(
            flops=2 * RANK * x.size + 2 * RANK * y.size, transcendentals=0, bytes_accessed=2 * (x.size + y.size)
        ),
    )(*args)


def factors(power):
    half = jnp.floor(power * 0.5)
    return jnp.exp2(half), jnp.exp2(power - half)


def coded(value):
    top = jnp.maximum(jnp.max(jnp.abs(value), 0, keepdims=True), 1e-37)
    power = jnp.floor(jnp.log2(top)) - 13.0
    first, second = factors(power)
    return jnp.round(value / first / second), power


def decoded(code, power):
    first, second = factors(power)
    return code * first * second


def spread_body(keep_ref, got_ref, s1_ref, s2_ref, s3_ref, in_ref, out_ref):
    x = lax.axis_index("x")
    out = keep_ref[NX * ROWS :] + got_ref[NX * ROWS :]
    out_ref[...] = out
    out_code, out_power = coded(out)
    line = lax.broadcasted_iota(I32, (ROWS, TOK), 0)
    for d, ref in ((1, s1_ref), (2, s2_ref), (3, s3_ref), (0, None)):
        at = pl.ds(pl.multiple_of((x ^ d) * ROWS, ROWS), ROWS)
        part = keep_ref[at, :] + got_ref[at, :]
        if ref is None:
            in_ref[...] = part
        else:
            code, power = coded(part)
            powers = jnp.where(line == 0, power, out_power)
            ref[...] = jnp.concatenate([code, out_code, powers], 0).astype(I32).astype(I16)


def join_body(first_ref, second_ref, out_ref):
    out_ref[: first_ref.shape[0]] = first_ref[...]
    out_ref[first_ref.shape[0] :] = second_ref[...]


def add_body(in_ref, out_ref, g2_ref, g1_ref, g3_ref, low_ref, half_ref):
    low, half = in_ref[...], out_ref[...]
    for ref in (g1_ref, g2_ref, g3_ref):
        got = ref[...].astype(I32).astype(F32)
        powers = got[ROWS + HALF :]
        low = low + decoded(got[:ROWS], powers[:1])
        half = half + decoded(got[ROWS : ROWS + HALF], powers[1:2])
    low_ref[...] = low
    half_ref[...] = half


def parts_of(value):
    high = value.astype(BF16)
    return high, (value - high.astype(F32)).astype(BF16)


def outer_body(in_ref, mine_ref, other_ref, where_ref, goal_ref, p_ref):
    core = lax.axis_index("core")
    low, mine, other = in_ref[...], mine_ref[...], other_ref[...]
    out = jnp.concatenate([jnp.where(core == 0, mine, other), jnp.where(core == 0, other, mine)], 0)
    out_high, out_low = parts_of(out)
    onehot = lax.broadcasted_iota(I32, (E_DEV, TOK), 0) == where_ref[...]
    pairs = [parts_of(jnp.where(onehot, low[i : i + 1], 0.0)) for i in range(ROWS)]
    high = jnp.concatenate([p[0] for p in pairs], 0)
    rest = jnp.concatenate([p[1] for p in pairs], 0)
    dot = lambda u, v: lax.dot_general(u, v, NT, preferred_element_type=F32)
    grads = dot(high, out_high) + (dot(high, out_low) + dot(rest, out_high))
    flat = [grads[i * E_DEV : (i + 1) * E_DEV] for i in range(ROWS)]
    goal = jnp.broadcast_to(goal_ref[...], (E_DEV, 128))
    goal = jnp.where(lax.broadcasted_iota(I32, (E_DEV, 128), 1) < 64, goal >> 4, goal & 15)
    p_ref[...] = jnp.concatenate(flat + [goal.astype(F32)], 1).astype(BF16)


def score_body(p0, p2, p1, p3, first_ref, second_ref, keep_ref, send_ref, goal_ref, held):
    core, z = lax.axis_index("core"), lax.axis_index("z")
    for m, bits in enumerate((0, 7, 2, 5, 1, 6, 3, 4)):
        at = pl.ds(pl.multiple_of((z ^ bits) * C_DEV, C_DEV), C_DEV)
        held[at, :] = (first_ref, second_ref)[m // (NZ // 2)][m % (NZ // 2)]
    ps = [p[...] for p in (p0, p1, p2, p3)]
    left = jnp.concatenate([p[:, :K_DEV] for p in ps], 0)
    score = lax.dot_general(left, held[...], NT, preferred_element_type=F32)
    first, second = score[:, :C_HALF], score[:, C_HALF:]
    keep_ref[...] = jnp.where(core == 0, first, second)
    send_ref[...] = jnp.where(core == 0, second, first)
    goal = jnp.concatenate([p[:, K_DEV:] for p in ps], 0).astype(F32)
    goal_ref[...] = jnp.broadcast_to(goal[:, :1] * 16.0 + goal[:, 64:65], (E_ALL, 128))


def pack_body(keep_ref, got_ref, code_ref):
    code, power = coded(keep_ref[...] + got_ref[...])
    power = jnp.broadcast_to(power, (2 * ROWS, C_HALF))
    code_ref[...] = jnp.concatenate([code, power], 0).astype(I32).astype(I16)


def sum_body(a0, a2, a1, a3, s0, s1, s2, s3):
    parts = []
    for ref in (a0, a1, a2, a3):
        got = ref[...].astype(I32).astype(F32)
        parts.append(decoded(got[:E_ALL], got[E_ALL : E_ALL + 1]))
    score = (parts[0] + parts[1]) + (parts[2] + parts[3])
    for d, ref in enumerate((s0, s1, s2, s3)):
        ref[...] = score[d * E_DEV : (d + 1) * E_DEV]


def total_body(s0, s1, s2, s3, goal_ref, slots_ref):
    core, y = lax.axis_index("core"), lax.axis_index("y")
    score = jnp.concatenate([s[...] for s in (s0, s1, s2, s3)], 0)
    first = ((y * NC + core) * C_HALF).astype(F32)
    goal = goal_ref[...] - first
    lane = lax.broadcasted_iota(I32, (E_ALL, 128), 1).astype(F32)
    pieces = []
    for j in range(C_HALF // 128):
        hit = goal == lane + 128.0 * j
        sums = jnp.sum(jnp.where(hit, score[:, 128 * j : 128 * (j + 1)], 0.0), 0, keepdims=True)
        pieces += [sums[:, i * C_DEV : (i + 1) * C_DEV] for i in range(128 // C_DEV) for _ in range(NC)]
    rows = jnp.concatenate(pieces, 0)
    for c in range(NC):
        slots_ref[c * len(pieces) : (c + 1) * len(pieces)] = jnp.where(core == c, rows, 0.0)


def lay_body(mine_ref, other_ref, flag_ref, out_ref):
    core, y = lax.axis_index("core"), lax.axis_index("y")
    for n, d in enumerate((0, 2, 1, 3)):
        for part, ref in ((core, mine_ref), (1 - core, other_ref)):
            at = pl.ds(pl.multiple_of((y ^ d) * C_ALL + part * C_HALF, C_HALF), C_HALF)
            out_ref[:, at] = ref[n * E_DEV : (n + 1) * E_DEV, :] * flag_ref[:, at].astype(F32)


def finish_body(slots_ref, own_flag_ref, total_ref):
    y, z = lax.axis_index("y"), lax.axis_index("z")
    flags = own_flag_ref[pl.ds(y * NZ + z, 1), :].astype(F32)
    total_ref[...] = jnp.sum(slots_ref[...], 0, keepdims=True) * flags


def per_device(
    down_matrix_feeds,
    result_slope_matrix,
    feed_sketch_factor,
    result_slope_factor,
    heldout_slope_entries,
    objective_of_sample,
    kept_choice_flags,
    token_sample_position,
):
    far = swap(heldout_slope_entries[None], "z", 7)
    keep, away, held = project(
        down_matrix_feeds,
        result_slope_matrix,
        feed_sketch_factor.T,
        result_slope_factor.T,
        heldout_slope_entries,
    )
    held = jnp.concatenate([held[None], far], 0)
    far = swap(held, "z", 2)

    sent = shaped(2 * ROWS + HALF, TOK, dtype=I16)
    low, half = shaped(ROWS, TOK), shaped(HALF, TOK)
    s1, s2, s3, in_own, out_chip = call(
        spread_body, [sent, sent, sent, low, half], keep, swap(away, "core", 1)
    )
    got = {d: swap(s, "x", d) for d, s in ((2, s2), (1, s1), (3, s3))}
    held = call(join_body, shaped(NZ // 2, C_DEV, K_DEV, dtype=BF16), held, far, after=in_own)
    far = swap(held, "z", 1)
    in_sum, out_half = call(add_body, [low, half], in_own, out_chip, got[2], got[1], got[3])
    packed = call(
        outer_body,
        shaped(E_DEV, K_DEV + 128, dtype=BF16),
        in_sum,
        out_half,
        swap(out_half, "core", 1),
        token_sample_position,
        objective_of_sample[:, None],
        work=400000000,
    )
    packs = {d: swap(packed, "y", d) for d in (2, 1, 3)}

    side = shaped(E_ALL, C_HALF)
    keep, send, goal = call(
        score_body,
        [side, side, shaped(E_ALL, 128)],
        packed,
        packs[2],
        packs[1],
        packs[3],
        held,
        far,
        scratch=[pltpu.VMEM((C_ALL, K_DEV), BF16)],
    )
    score = call(
        pack_body, shaped(E_ALL + 2 * ROWS, C_HALF, dtype=I16), keep, swap(send, "core", 1)
    )
    got = {d: swap(score, "x", d) for d in (2, 1, 3)}
    piece = shaped(E_DEV, C_HALF)
    pieces = call(sum_body, [piece] * NY, score, got[2], got[1], got[3])
    slots = call(total_body, shaped(NZ * NC, C_DEV), *pieces, goal)
    got = {d: swap(pieces[d], "y", d) for d in (2, 1, 3)}
    mine = jnp.concatenate([pieces[0], got[2], got[1], got[3]], 0)
    mine, slots = lax.optimization_barrier((mine, slots))
    sample_affinity = call(
        lay_body,
        shaped(E_DEV, CHOICES),
        mine,
        swap(mine, "core", 1),
        kept_choice_flags.reshape(1, CHOICES),
    )
    totals = call(
        finish_body,
        shaped(1, C_DEV),
        lax.all_to_all(slots, ("z", "core"), 0, 0, tiled=True),
        kept_choice_flags.reshape(NY * NZ, C_DEV),
        after=sample_affinity,
    )
    return (sample_affinity, totals[0])


def solution(mesh):
    ex, tp = ("y", "z"), ("x", "core")
    chips = Mesh(mesh.devices.reshape(NY, NZ, NX, NC), ("y", "z", "x", "core"))
    placed = (
        P(ex, tp),
        P(ex, tp),
        P(tp, None),
        P(tp, None),
        P(ex, tp),
        P(ex),
        P(),
        P(ex, None),
    )
    return jax.shard_map(
        per_device, mesh=chips, in_specs=placed, out_specs=(P(ex, None), P(ex)), check_vma=False
    )
```
